256 devices in a mesh: gx: 4 (over x), gy: 4 (over y), gz: 16 (over z, core).
Axes of the slice: x: 4, y: 4, z: 8, core: 2. Of those that a mesh axis runs over, the one named last changes fastest.
Arguments:
- rhs_fine: float32 [32, 128, 8192], P('gx', 'gy', 'gz'), may hold values from -8 to 8
- beta_fine: float32 [32, 128, 8192], P('gx', 'gy', 'gz'), may hold values from 0.1 to 10
- rhs_mid: float32 [16, 64, 4096], P('gx', 'gy', 'gz'), may hold values from -8 to 8
- beta_mid: float32 [16, 64, 4096], P('gx', 'gy', 'gz'), may hold values from 0.1 to 10
- rhs_coarse: float32 [8, 32, 2048], P('gx', 'gy', 'gz'), may hold values from -8 to 8
- beta_coarse: float32 [8, 32, 2048], P('gx', 'gy', 'gz'), may hold values from 0.1 to 10
Outputs:
- corr_fine: float32 [32, 128, 8192], P('gx', 'gy', 'gz')
- corr_coarse: float32 [8, 32, 2048], P('gx', 'gy', 'gz')
The draws below stay inside these ranges and needn't reach their ends.
All inputs are finite; a program needn't handle non-finite values.
Results may differ from the reference program's by a relative error of at most 0.0003.
Values sent between devices are 32-bit elements; how exact they have to be, the bound alone decides.
No kernel may reach another device: no remote copies, remote signals or barrier semaphores. Data moves between devices by JAX's collectives and lax.ppermute only.
A program may use at most 128 MiB of HBM per device.

```python
import math
import jax
import jax.numpy as jnp

ITERS = 8
SWEEPS = 2
NX0 = 32
NY0 = 128
NZ0 = 8192
NX1 = 16
NY1 = 64
NZ1 = 4096
NX2 = 8
NY2 = 32
NZ2 = 2048


def shard_levels(own_key, extent, cuts, smallest, largest):
    factor_of = 1.0
    for position, blocks in cuts:
        steps = jax.random.uniform(jax.random.fold_in(jax.random.fold_in(own_key, 6), position), (blocks,), jnp.float32, smallest / len(cuts), largest / len(cuts))
        factor_of = factor_of * jnp.repeat(jnp.exp(steps), extent[position] // blocks).reshape((-1,) + (1,) * (len(extent) - 1 - position))
    return factor_of


def normal_values(own_key, extent, deviation, limit, shards=(), dtype=jnp.bfloat16):
    result = jax.random.normal(own_key, extent, jnp.float32) * deviation
    if len(shards) > 0:
        result = shard_levels(own_key, extent, shards, -0.22, 0.18) * result
    return jnp.clip(result, min=-limit, max=limit).astype(dtype)


def setup_inputs(seed: int = 0) -> dict:
    seeds = jax.random.split(jax.random.key(seed), 7)
    return {
        "rhs_fine": normal_values(seeds[0], (NX0, NY0, NZ0), 1.0, 8.0, ((0, 4), (1, 4), (2, 16)), jnp.float32),
        "beta_fine": jnp.clip(jnp.exp(math.log(10.0) - 4.6051702 * jax.random.uniform(seeds[1], (NX0, NY0, NZ0), jnp.float32) ** shard_levels(seeds[1], (NX0, NY0, NZ0), ((0, 4), (1, 4), (2, 16)), -0.2, 0.2)), 0.1, 10.0),
        "rhs_mid": normal_values(seeds[2], (NX1, NY1, NZ1), 1.0, 8.0, ((0, 4), (1, 4), (2, 16)), jnp.float32),
        "beta_mid": jnp.clip(jnp.exp(math.log(10.0) - 4.6051702 * jax.random.uniform(seeds[3], (NX1, NY1, NZ1), jnp.float32) ** shard_levels(seeds[3], (NX1, NY1, NZ1), ((0, 4), (1, 4), (2, 16)), -0.2, 0.2)), 0.1, 10.0),
        "rhs_coarse": normal_values(seeds[4], (NX2, NY2, NZ2), 1.0, 8.0, ((0, 4), (1, 4), (2, 16)), jnp.float32),
        "beta_coarse": jnp.clip(jnp.exp(math.log(10.0) - 4.6051702 * jax.random.uniform(seeds[5], (NX2, NY2, NZ2), jnp.float32) ** shard_levels(seeds[5], (NX2, NY2, NZ2), ((0, 4), (1, 4), (2, 16)), -0.2, 0.2)), 0.1, 10.0),
    }


def neighbours(padded):
    return [padded[2:, 1:-1, 1:-1], padded[:-2, 1:-1, 1:-1], padded[1:-1, 2:, 1:-1], padded[1:-1, :-2, 1:-1], padded[1:-1, 1:-1, 2:], padded[1:-1, 1:-1, :-2]]


def couple(value_pad, beta_pad):
    centre = beta_pad[1:-1, 1:-1, 1:-1]
    diag = jnp.zeros_like(centre)
    off = jnp.zeros_like(centre)
    for beta_n, value_n in zip(neighbours(beta_pad), neighbours(value_pad)):
        weight = 0.5 * (centre + beta_n)
        diag = diag + weight
        off = off + weight * value_n
    return diag, off


def refine(field):
    a, b, c = field.shape
    return jnp.broadcast_to(field[:, None, :, None, :, None], (a, 2, b, 2, c, 2)).reshape(2 * a, 2 * b, 2 * c)


def parity_of(shape):
    ix = jax.lax.broadcasted_iota(jnp.int32, shape, 0)
    iy = jax.lax.broadcasted_iota(jnp.int32, shape, 1)
    iz = jax.lax.broadcasted_iota(jnp.int32, shape, 2)
    return (ix + iy + iz) % 2


def relax(field, rhs, beta):
    beta_pad = jnp.pad(beta, 1)
    parity = parity_of(field.shape)
    for sweep in range(SWEEPS):
        for colour in (0, 1):
            diag, off = couple(jnp.pad(field, 1), beta_pad)
            field = jnp.where(parity == colour, (rhs + off) / diag, field)
    return field


def reference(rhs_fine, beta_fine, rhs_mid, beta_mid, rhs_coarse, beta_coarse):
    beta_pad = jnp.pad(beta_coarse, 1)

    def operate(vec):
        diag, off = couple(jnp.pad(vec, 1), beta_pad)
        return diag * vec - off

    x = jnp.zeros_like(rhs_coarse)
    r = rhs_coarse
    rhat = rhs_coarse
    p = r
    rho = jnp.sum(rhat * r)
    for step in range(ITERS):
        v = operate(p)
        alpha = rho / jnp.sum(rhat * v)
        s = r - alpha * v
        t = operate(s)
        omega = jnp.sum(t * s) / jnp.sum(t * t)
        x = x + alpha * p + omega * s
        r = s - omega * t
        rho_new = jnp.sum(rhat * r)
        p = r + (rho_new / rho) * (alpha / omega) * (p - omega * v)
        rho = rho_new
    corr_coarse = x
    field = relax(refine(corr_coarse), rhs_mid, beta_mid)
    field = relax(refine(field), rhs_fine, beta_fine)
    return field, corr_coarse
```

```python
import jax
import jax.numpy as jnp
from jax import lax
from jax.experimental import pallas as pl
from jax.experimental.pallas import tpu as pltpu
from jax.sharding import PartitionSpec as P

ITERS = 8
SWEEPS = 2
F32 = jnp.float32
VREG = (8, 128)

NX, NJ, NK = 8, 4, 16
KC = 2

FY, FZ = 5, 5
MY, MZ = 4, 3
FT, MT = FY * FZ, MY * MZ
PAIRS = 8
F_SEND = 4 * 2 * FT
SEND = F_SEND + 4 * 2 * MT
SHIFTS = (0, 1, 3, 2)


def iota(dim):
    return lax.broadcasted_iota(jnp.int32, VREG, dim)


def params(mib):
    return pltpu.CompilerParams(vmem_limit_bytes=mib * 2**20)


def tiles(n):
    return jax.ShapeDtypeStruct((n,) + VREG, F32)


def pack_coarse_kernel(rhs, beta, out, scratch):
    for arr, ref in enumerate((rhs, beta)):
        for xi in range(2):
            block = jnp.concatenate([ref[xi], jnp.zeros((120, 128), F32)], axis=0)
            scratch[...] = block.T
            lane = iota(1)
            acc = jnp.zeros(VREG, F32)
            for zlo in range(16):
                rows = scratch[pl.ds(zlo, 8, stride=16), :]
                if zlo:
                    rows = pltpu.roll(rows, 8 * zlo, 1)
                acc = jnp.where(lane // 8 == zlo, rows, acc)
            out[arr * 2 + xi] = acc


def pack_coarse(rhs, beta):
    return pl.pallas_call(
        pack_coarse_kernel,
        out_shape=tiles(4),
        scratch_shapes=[pltpu.VMEM((128, 128), F32)],
        name="pack_coarse",
    )(rhs, beta)


def pack_z_kernel(*refs):
    ins, outs = refs[:8], refs[8:]
    for side in range(2):
        at = 0
        for ref in ins[side * 4 : side * 4 + 4]:
            planes, rows, _ = ref.shape
            for x in range(planes):
                for yt in range(rows // 8):
                    outs[side][at] = ref[x, yt * 8 : yt * 8 + 8, :]
                    at += 1


def pack_z(fine, mid):
    specs, args = [], []
    for last in (0, 1):
        for a in fine + mid:
            x, y, z = a.shape
            block = (z // 128 - 1) * last
            specs.append(pl.BlockSpec((x, y, 128), lambda i, block=block: (0, 0, block)))
            args.append(a)
    whole = pl.BlockSpec((80,) + VREG, lambda i: (0, 0, 0))
    return pl.pallas_call(
        pack_z_kernel,
        grid=(1,),
        in_specs=specs,
        out_specs=(whole, whole),
        out_shape=(tiles(80), tiles(80)),
        name="pack_z",
    )(*args)


def pack_y_kernel(*refs):
    ins, (nxt, prv), (zh, first, last) = refs[:8], refs[8:10], refs[10:]
    right = iota(1) < 64
    for at in range(80):
        zh[at] = jnp.where(right, nxt[at], prv[at])
    for side, out in enumerate((first, last)):
        at = 0
        for n, ref in enumerate(ins[side * 4 : side * 4 + 4]):
            planes, _, lanes = ref.shape
            zts = lanes // 128
            for x in range(planes):
                for zt in range(zts):
                    out[at] = ref[x, :, zt * 128 : zt * 128 + 128]
                    at += 1
                if n < 2:
                    out[at] = zh[(n * 8 + x) * 4 + 3 * side]
                else:
                    out[at] = zh[64 + ((n - 2) * 4 + x) * 2 + side]
                at += 1


def pack_y(fine, mid, nxt, prv):
    specs, args = [], []
    for last in (0, 1):
        for a in fine + mid:
            x, y, z = a.shape
            block = (y // 8 - 1) * last
            specs.append(pl.BlockSpec((x, 8, z), lambda i, block=block: (0, block, 0)))
            args.append(a)
    n = 2 * 8 * FZ + 2 * 4 * MZ
    eighty = pl.BlockSpec((80,) + VREG, lambda i: (0, 0, 0))
    rows = pl.BlockSpec((n,) + VREG, lambda i: (0, 0, 0))
    return pl.pallas_call(
        pack_y_kernel,
        grid=(1,),
        in_specs=specs + [eighty, eighty],
        out_specs=(eighty, rows, rows),
        out_shape=(tiles(80), tiles(n), tiles(n)),
        name="pack_y",
    )(*args, nxt, prv)


def pack_x_kernel(rf, bf, rm, bm, zh, nxt, prv, down, up, down2, up2):
    below = iota(0) < 4

    def fine_plane(x, out, p):
        for a, ref in enumerate((rf, bf)):
            base = (p * 2 + a) * FT
            for yt in range(4):
                for zt in range(4):
                    out[base + yt * FZ + zt] = ref[x, yt * 8 : yt * 8 + 8, zt * 128 : zt * 128 + 128]
                out[base + yt * FZ + 4] = zh[(a * 8 + x) * 4 + yt]
            for zt in range(FZ):
                at = (a * 8 + x) * FZ + zt
                out[base + 4 * FZ + zt] = jnp.where(below, nxt[at], prv[at])

    for p in range(4):
        fine_plane(p, down, p)
        fine_plane(p + 4, up, p)
        for a, ref in enumerate((rm, bm)):
            plane = []
            for yt in range(2):
                for zt in range(2):
                    plane.append(ref[p, yt * 8 : yt * 8 + 8, zt * 128 : zt * 128 + 128])
                plane.append(zh[64 + (a * 4 + p) * 2 + yt])
            for side in (nxt, prv):
                for zt in range(MZ):
                    plane.append(side[2 * 8 * FZ + (a * 4 + p) * MZ + zt])
            for i, tile in enumerate(plane):
                down[F_SEND + (p * 2 + a) * MT + i] = tile
                up[F_SEND + (p * 2 + a) * MT + i] = tile
                if p < 2:
                    down2[(p * 2 + a) * MT + i] = tile
                else:
                    up2[((p - 2) * 2 + a) * MT + i] = tile


def pack_x(fine, mid, zh, nxt, prv):
    return pl.pallas_call(
        pack_x_kernel,
        out_shape=(tiles(SEND), tiles(SEND), tiles(4 * MT), tiles(4 * MT)),
        compiler_params=params(32),
        name="pack_x",
    )(*fine, *mid, zh, nxt, prv)


def join_kernel(y_on_first_core, *refs):
    ins, out = refs[:4], refs[4]
    gx, gy, gz = lax.axis_index("gx"), lax.axis_index("gy"), lax.axis_index("gz")
    along_y = (lax.rem(gz, 2) == 0) == y_on_first_core
    mine = jnp.where(along_y, gy, gx)
    for step, ref in zip(SHIFTS, ins):
        slot = lax.rem(mine + 4 - step, 4)

        def copy(i, _, slot=slot, ref=ref):
            for part in range(4):
                out[slot, i, part] = ref[i, part]
            return 0

        lax.fori_loop(0, ref.shape[0], copy, 0, unroll=8)


def join(parts, y_on_first_core):
    n = parts[0].shape[0]
    return pl.pallas_call(
        lambda *refs: join_kernel(y_on_first_core, *refs),
        out_shape=jax.ShapeDtypeStruct((4, n, 4) + VREG, F32),
        compiler_params=params(16),
        name="join",
    )(*parts)


def gather(part, y_on_first_core):
    def device(x, y, z):
        return (x % 4 * 4 + y % 4) * 16 + z

    parts = [part]
    for step in SHIFTS[1:]:
        pairs = []
        for x in range(4):
            for y in range(4):
                for z in range(16):
                    along_y = (z % 2 == 0) == y_on_first_core
                    to = device(x, y + step, z) if along_y else device(x + step, y, z)
                    pairs.append((device(x, y, z), to))
        parts.append(lax.ppermute(part, ("gx", "gy", "gz"), pairs))
    return parts


def solve_kernel(own, other, window, y_nat, beta, rhat, r, v, t, x, vp, vs, wx, wy, wz, nat):
    gx, gy, gz = lax.axis_index("gx"), lax.axis_index("gy"), lax.axis_index("gz")
    lane, sub = iota(1), iota(0)
    first_core = lax.rem(gz, 2) == 0

    for arr, dest in ((0, rhat), (1, beta)):

        def unpack(i, _, arr=arr, dest=dest):
            xx, by = i // 4, lax.rem(i, 4)
            bx = xx // 2
            part = arr * 2 + lax.rem(xx, 2)
            outer, inner = jnp.where(first_core, bx, by), jnp.where(first_core, by, bx)
            rows = []
            for chip in range(8):
                a, b = own[outer, inner * 8 + chip, part], other[inner, outer * 8 + chip, part]
                rows += [jnp.where(first_core, a, b), jnp.where(first_core, b, a)]
            block = jnp.concatenate(rows, axis=0).T
            for k in range(NK):
                y_nat[xx, k, pl.ds(pl.multiple_of(by * 8, 8), 8), :] = block[k * 8 : k * 8 + 8]
            return 0

        lax.fori_loop(0, 32, unpack, 0)

        def interleave(xx, _, arr=arr, dest=dest):
            for k in range(NK):
                for j in range(NJ):
                    tile = y_nat[xx, k, pl.ds(j, 8, stride=4), :]
                    dest[xx, j, k] = tile if arr == 0 else 0.5 * tile
            return 0

        lax.fori_loop(0, NX, interleave, 0)

    def shift_up(a):
        return jnp.where(sub == 0, 0.0, pltpu.roll(a, 1, 0))

    def shift_down(a):
        return jnp.where(sub == 7, 0.0, pltpu.roll(a, 7, 0))

    def shift_right(a):
        return jnp.where(lane == 0, 0.0, pltpu.roll(a, 1, 1))

    def shift_left(a):
        return jnp.where(lane == 127, 0.0, pltpu.roll(a, 127, 1))

    wx[0] = beta[0]
    wx[NX] = beta[NX - 1]

    def faces(xx, _):
        @pl.when(xx > 0)
        def _():
            for j in range(NJ):
                for k in range(NK):
                    wx[xx, j, k] = beta[xx - 1, j, k] + beta[xx, j, k]

        for k in range(NK):
            col = [beta[xx, j, k] for j in range(NJ)]
            col = [shift_up(col[3])] + col + [shift_down(col[0])]
            for j in range(NJ + 1):
                wy[xx, j, k] = col[j] + col[j + 1]
        for j in range(NJ):
            row = [beta[xx, j, k] for k in range(NK)]
            row = [shift_right(row[15])] + row + [shift_left(row[0])]
            for k in range(NK + 1):
                wz[xx, j, k] = row[k] + row[k + 1]
        return 0

    lax.fori_loop(0, NX, faces, 0)

    def put(vec, xx, j, k, value):
        vec[xx + 1, j, k + 1] = value
        if k == 0:
            vec[xx + 1, j, NK + 1] = shift_left(value)
        if k == NK - 1:
            vec[xx + 1, j, 0] = shift_right(value)

    def total(acc):
        out = acc[0]
        for a in acc[1:]:
            out = out + a
        return jnp.broadcast_to(jnp.sum(out, keepdims=True), VREG)

    CELLS = [(j, k) for j in range(NJ) for k in range(KC)]

    def operate(vec, out, sums):
        def body(i, acc):
            k0 = i * KC
            acc = list(acc)
            centre = {c: vec[1, c[0], k0 + 1 + c[1]] for c in CELLS}
            low = {c: wx[0, c[0], k0 + c[1]] * centre[c] for c in CELLS}
            for xx in range(NX):
                if xx + 1 < NX:
                    after = {c: vec[xx + 2, c[0], k0 + 1 + c[1]] for c in CELLS}
                    high = {c: wx[xx + 1, c[0], k0 + c[1]] * (after[c] - centre[c]) for c in CELLS}
                else:
                    after = None
                    high = {c: -(wx[xx + 1, c[0], k0 + c[1]] * centre[c]) for c in CELLS}
                value = {c: low[c] - high[c] for c in CELLS}
                for k in range(KC):
                    col = [centre[j, k] for j in range(NJ)]
                    col = [shift_up(col[3])] + col + [shift_down(col[0])]
                    flux = [wy[xx, j, k0 + k] * (col[j + 1] - col[j]) for j in range(NJ + 1)]
                    for j in range(NJ):
                        value[j, k] = value[j, k] + (flux[j] - flux[j + 1])
                for j in range(NJ):
                    row = [vec[xx + 1, j, k0]] + [centre[j, k] for k in range(KC)] + [vec[xx + 1, j, k0 + KC + 1]]
                    flux = [wz[xx, j, k0 + k] * (row[k + 1] - row[k]) for k in range(KC + 1)]
                    for k in range(KC):
                        value[j, k] = value[j, k] + (flux[k] - flux[k + 1])
                for c in CELLS:
                    out[xx, c[0], k0 + c[1]] = value[c]
                    terms = sums(value[c], centre[c], rhat[xx, c[0], k0 + c[1]])
                    slot = c[1]
                    for n, term in enumerate(terms):
                        acc[n * KC + slot] = acc[n * KC + slot] + term
                centre, low = after, high
            return tuple(acc)

        zero = jnp.zeros(VREG, F32)
        n = len(sums(zero, zero, zero))
        acc = lax.fori_loop(0, NK // KC, body, (zero,) * (n * KC))
        return [total(acc[m * KC : m * KC + KC]) for m in range(n)]

    def start(xx, acc):
        for j in range(NJ):
            for k in range(NK):
                a = rhat[xx, j, k]
                r[xx, j, k] = a
                put(vp, xx, j, k, a)
                acc = acc + a * a
        return acc

    rho = total([lax.fori_loop(0, NX, start, jnp.zeros(VREG, F32))])

    for step in range(ITERS):
        (rv,) = operate(vp, v, lambda av, _, rh: (rh * av,))
        alpha = rho / rv

        def half(xx, _):
            for j in range(NJ):
                for k in range(NK):
                    put(vs, xx, j, k, r[xx, j, k] - alpha * v[xx, j, k])
            return 0

        lax.fori_loop(0, NX, half, 0)
        ts, tt, rt = operate(vs, t, lambda at, s, rh: (at * s, at * at, rh * at))
        omega = ts / tt
        rho_new = -omega * rt
        scale = rho_new / rho * (alpha / omega)

        def update(xx, _, step=step, alpha=alpha, omega=omega, scale=scale):
            for j in range(NJ):
                for k in range(NK):
                    p, s = vp[xx + 1, j, k + 1], vs[xx + 1, j, k + 1]
                    gain = alpha * p + omega * s
                    x[xx, j, k] = gain if step == 0 else x[xx, j, k] + gain
                    if step < ITERS - 1:
                        res = s - omega * t[xx, j, k]
                        r[xx, j, k] = res
                        put(vp, xx, j, k, res + scale * (p - omega * v[xx, j, k]))
            return 0

        lax.fori_loop(0, NX, update, 0)
        rho = rho_new

    first = lax.rem(128 + 8 * gz - 2, 128)

    def extract(i, _):
        xx = jnp.clip(2 * gx - 3 + i, 0, NX - 1)
        for h in range(2):
            nat[h, 0:8, :] = jnp.zeros(VREG, F32)
            nat[h, 40:48, :] = jnp.zeros(VREG, F32)
            for j in range(NJ):
                acc = jnp.zeros(VREG, F32)
                for kk in range(8):
                    rolled = pltpu.roll(x[xx, j, h * 8 + kk], lax.rem(16 * kk + 128 - first, 128), 1)
                    acc = jnp.where(lane // 16 == kk, rolled, acc)
                nat[h, pl.ds(8 + j, 8, stride=4), :] = acc
            for tile, row in enumerate((8 * gy + 8, 8 * gy + 16, 8 * gy)):
                window[i, tile, h] = nat[h, pl.ds(pl.multiple_of(row, 8), 8), :]
        return 0

    lax.fori_loop(0, 8, extract, 0)


def solve(own, other):
    full = pltpu.VMEM((NX, NJ, NK) + VREG, F32)
    vector = pltpu.VMEM((NX + 2, NJ, NK + 2) + VREG, F32)
    return pl.pallas_call(
        solve_kernel,
        out_shape=jax.ShapeDtypeStruct((8, 3, 2) + VREG, F32),
        scratch_shapes=[pltpu.VMEM((NX, NK, 32, 128), F32)]
        + [full] * 6
        + [
            vector,
            vector,
            pltpu.VMEM((NX + 1, NJ, NK) + VREG, F32),
            pltpu.VMEM((NX, NJ + 1, NK) + VREG, F32),
            pltpu.VMEM((NX, NJ, NK + 1) + VREG, F32),
            pltpu.VMEM((2, 48, 128), F32),
        ],
        compiler_params=params(52),
        cost_estimate=pl.CostEstimate(flops=400_000_000, bytes_accessed=100_000_000, transcendentals=0),
        name="solve",
    )(own, other)


def level_helpers(ny, nz):
    lane, sub = iota(1), iota(0)

    def up_rolled(row):
        return [pltpu.roll(p, 1, 0) for p in row]

    def down_rolled(row):
        return [pltpu.roll(p, 7, 0) for p in row]

    def from_above(edge, here):
        return [jnp.where(sub == 0, p, q) for p, q in zip(edge, here)]

    def from_below(edge, here):
        return [jnp.where(sub == 7, p, q) for p, q in zip(edge, here)]

    def from_left(row):
        rolled = [pltpu.roll(p, 1, 1) for p in row]
        return [jnp.where(lane == 0, rolled[b - 1], rolled[b]) for b in range(nz)]

    def from_right(row):
        rolled = [pltpu.roll(p, 127, 1) for p in row]
        return [jnp.where(lane == 127, rolled[(b + 1) % nz], rolled[b]) for b in range(nz)]

    def load(ref, m, a):
        return [ref[m, (a % ny) * nz + b] for b in range(nz)]

    return up_rolled, down_rolled, from_above, from_below, from_left, from_right, load


def prepare_level(w, ny, nz, inside):
    up_rolled, down_rolled, from_above, from_below, from_left, from_right, load = level_helpers(ny, nz)
    even = lax.rem(iota(0) + iota(1), 2) == 0

    def body(m, _):
        before, after = jnp.maximum(m - 1, 0), jnp.minimum(m + 1, PAIRS - 1)
        last = [up_rolled(load(w.b[c], m, ny - 1)) for c in (0, 1)]
        first = waiting = None

        def finish(a, diag, here, edge):
            for c in (0, 1):
                high = from_below(edge[1 - c], here[1 - c])
                for b in range(nz):
                    i = a * nz + b
                    w.inv[c][m, i] = jnp.where(inside(m, i), 1.0 / (diag[c][b] + high[b]), 0.0)

        for a in range(ny):
            rows = [load(w.b[c], m, a) for c in (0, 1)]
            rolled = [up_rolled(rows[c]) for c in (0, 1)]
            low_y = [[p + q for p, q in zip(rows[c], from_above(last[1 - c], rolled[1 - c]))] for c in (0, 1)]
            last = rolled
            low_z = [[p + q for p, q in zip(rows[c], from_left(rows[1 - c]))] for c in (0, 1)]
            diag = []
            for c in (0, 1):
                high_z = from_right(low_z[1 - c])
                total = []
                for b in range(nz):
                    i = a * nz + b
                    x_in = rows[0][b] + rows[1][b]
                    lower, upper = w.b[1 - c][before, i], w.b[1 - c][after, i]
                    x_out = rows[c][b] + (jnp.where(even, lower, upper) if c == 0 else jnp.where(even, upper, lower))
                    if c == 0:
                        w.x_in[m, i] = x_in
                    w.x_out[c][m, i] = x_out
                    w.y[c][m, i] = low_y[c][b]
                    w.z[c][m, i] = low_z[c][b]
                    total.append((x_in + x_out) + low_y[c][b] + (low_z[c][b] + high_z[b]))
                diag.append(total)
            here = [down_rolled(low_y[c]) for c in (0, 1)]
            if a == 0:
                first = here
            else:
                finish(a - 1, waiting[0], waiting[1], here)
            waiting = (diag, here)
        finish(ny - 1, waiting[0], waiting[1], first)
        return 0

    lax.fori_loop(0, PAIRS, body, 0)


def smooth_level(w, ny, nz):
    up_rolled, down_rolled, from_above, from_below, from_left, from_right, load = level_helpers(ny, nz)
    even = lax.rem(iota(0) + iota(1), 2) == 0

    for half in range(2 * SWEEPS):
        c = half % 2
        old, new = w.e[1 - c], w.e[c]

        def body(m, _, c=c, old=old, new=new):
            before, after = jnp.maximum(m - 1, 0), jnp.minimum(m + 1, PAIRS - 1)

            def lowered(a, row):
                return down_rolled([p * q for p, q in zip(load(w.y[1 - c], m, a), row)])

            last = up_rolled(load(old, m, ny - 1))
            row = load(old, m, 0)
            here = first = lowered(0, row)
            for a in range(ny):
                rolled = up_rolled(row)
                up = from_above(last, rolled)
                if a + 1 < ny:
                    row_next = load(old, m, a + 1)
                    edge = lowered(a + 1, row_next)
                else:
                    row_next, edge = None, first
                down = from_below(edge, here)
                left = from_left(row)
                right = from_right([p * q for p, q in zip(load(w.z[1 - c], m, a), row)])
                for b in range(nz):
                    i = a * nz + b
                    lower, upper = old[before, i], old[after, i]
                    far = jnp.where(even, lower, upper) if c == 0 else jnp.where(even, upper, lower)
                    off = w.x_in[m, i] * row[b] + w.x_out[c][m, i] * far
                    off = off + (w.y[c][m, i] * up[b] + down[b]) + (w.z[c][m, i] * left[b] + right[b])
                    new[m, i] = (w.r[c][m, i] + off) * w.inv[c][m, i]
                last, row, here = rolled, row_next, edge
            return 0

        skip = (half + 1) // 2
        lax.fori_loop(skip, PAIRS - skip, body, 0)


class Level:
    def __init__(self, refs):
        refs = list(refs)
        self.x_in = refs[0]
        self.e, self.r, self.b, self.x_out, self.y, self.z, self.inv = (refs[1 + 2 * i : 3 + 2 * i] for i in range(7))


def smooth_kernel(window, down, up, nxt, prv, nxt2, prv2, out_fine, out_coarse, *scratch):
    gx, gy, gz = lax.axis_index("gx"), lax.axis_index("gy"), lax.axis_index("gz")
    lane, sub = iota(1), iota(0)
    even = lax.rem(lane + sub, 2) == 0
    mid, fine = Level(scratch[:15]), Level(scratch[15:])

    def place(ref, base, n, level, pair0, pairs):
        def copy(p, _):
            at = base + p * 4 * n
            for i in range(n):
                for kind, dest, scale in ((0, level.r, None), (1, level.b, 0.5)):
                    one, two = ref[at + kind * n + i], ref[at + 2 * n + kind * n + i]
                    if scale:
                        one, two = scale * one, scale * two
                    dest[0][pair0 + p, i] = jnp.where(even, one, two)
                    dest[1][pair0 + p, i] = jnp.where(even, two, one)
            return 0

        lax.fori_loop(0, pairs, copy, 0)

    place(prv2, 0, MT, mid, 0, 1)
    place(prv, F_SEND, MT, mid, 1, 2)
    place(down, F_SEND, MT, mid, 3, 2)
    place(nxt, F_SEND, MT, mid, 5, 2)
    place(nxt2, 0, MT, mid, 7, 1)
    place(prv, 0, FT, fine, 0, 2)
    place(down, 0, FT, fine, 2, 2)
    place(up, 0, FT, fine, 4, 2)
    place(nxt, 0, FT, fine, 6, 2)

    everywhere = jnp.full(VREG, True)
    in_z = ((lane < 64) & (gz < 15)) | ((lane >= 64) & (gz > 0))
    in_y = ((sub < 4) & (gy < 3)) | ((sub >= 4) & (gy > 0))

    def inside_x(m, first, size):
        return (2 * m + first >= 0) & (2 * m + first < size)

    def mid_inside(m, i):
        yt, zt = i // MZ, i % MZ
        y = everywhere if yt < 2 else jnp.full(VREG, gy < 3 if yt == 2 else gy > 0)
        return y & (everywhere if zt < 2 else in_z) & inside_x(m, 4 * gx - 6, 16)

    def fine_inside(m, i):
        yt, zt = i // FZ, i % FZ
        return (in_y if yt == 4 else everywhere) & (in_z if zt == 4 else everywhere) & inside_x(m, 8 * gx - 4, 32)

    prepare_level(mid, MY, MZ, mid_inside)
    prepare_level(fine, FY, FZ, fine_inside)

    src = lax.broadcasted_iota(jnp.int32, (256, 512), 0)
    dst = lax.broadcasted_iota(jnp.int32, (256, 512), 1)
    cell = 16 * (src % 16 - 2) + src // 16
    lanes = jnp.where(dst >= 320, dst - 384, dst)
    wanted = jnp.where(dst >= 384, dst - 384, (lanes + 128) // 2 - 64)
    pick = (cell == wanted).astype(F32)
    source = jnp.concatenate(
        [
            jnp.concatenate([window[i, tile, 0], window[i, tile, 1]], axis=1)
            for i in range(8)
            for tile in range(3)
        ],
        axis=0,
    )
    wide = jnp.dot(source, pick, precision=lax.Precision.HIGHEST, preferred_element_type=F32)

    def tile_of(i, tile, zt):
        row = (i * 3 + tile) * 8
        return wide[row : row + 8, zt * 128 : zt * 128 + 128]

    for i in range(2):
        out_coarse[i] = tile_of(3 + i, 0, 3)

    def doubled_rows(a, half):
        return jnp.take_along_axis(a, sub // 2 + 4 * half, axis=0, mode="promise_in_bounds")

    def doubled_lanes(a, half):
        return jnp.take_along_axis(a, lane // 2 + 64 * half, axis=1, mode="promise_in_bounds")

    for i in range(8):
        for zt in range(MZ):
            plane = [
                doubled_rows(tile_of(i, 0, zt), 0),
                doubled_rows(tile_of(i, 0, zt), 1),
                doubled_rows(tile_of(i, 1, zt), 0),
                doubled_rows(tile_of(i, 2, zt), 1),
            ]
            for yt in range(MY):
                mid.e[1][i, yt * MZ + zt] = jnp.where(mid_inside(i, yt * MZ + zt), plane[yt], 0.0)

    smooth_level(mid, MY, MZ)

    def prolong(pair, _):
        for odd in range(2):
            plane = []
            for b in range(MZ):
                src = []
                for a in range(MY):
                    red, black = (mid.e[c][pair + 2, a * MZ + b] for c in (0, 1))
                    src.append(jnp.where(even, black, red) if odd else jnp.where(even, red, black))
                edge = jnp.where(sub < 4, doubled_rows(src[2], 0), doubled_rows(src[3], 1))
                plane.append([doubled_rows(src[a // 2], a % 2) for a in range(4)] + [edge])
            for a in range(FY):
                row = [doubled_lanes(plane[b // 2][a], b % 2) for b in range(4)]
                last = plane[2][a]
                row.append(jnp.where(lane < 64, doubled_lanes(last, 0), doubled_lanes(last, 1)))
                for b in range(FZ):
                    fine.e[1][2 * pair + odd, a * FZ + b] = row[b]
        return 0

    lax.fori_loop(0, 4, prolong, 0)
    smooth_level(fine, FY, FZ)

    def store(p, _):
        for a in range(4):
            for b in range(4):
                red, black = (fine.e[c][p + 2, a * FZ + b] for c in (0, 1))
                out_fine[2 * p, a * 8 : a * 8 + 8, b * 128 : b * 128 + 128] = jnp.where(even, red, black)
                out_fine[2 * p + 1, a * 8 : a * 8 + 8, b * 128 : b * 128 + 128] = jnp.where(even, black, red)
        return 0

    lax.fori_loop(0, 4, store, 0)


def smooth(window, *parts):
    mid = pltpu.VMEM((PAIRS, MT) + VREG, F32)
    fine = pltpu.VMEM((PAIRS, FT) + VREG, F32)
    return pl.pallas_call(
        smooth_kernel,
        out_shape=(jax.ShapeDtypeStruct((8, 32, 512), F32), jax.ShapeDtypeStruct((2,) + VREG, F32)),
        scratch_shapes=[mid] * 15 + [fine] * 15,
        compiler_params=params(48),
        name="smooth",
    )(window, *parts)


def send(a, axis, step):
    n = lax.axis_size(axis)
    return lax.ppermute(a, axis, [(i, i + step) for i in range(n) if 0 <= i + step < n])


def shards(rhs_fine, beta_fine, rhs_mid, beta_mid, rhs_coarse, beta_coarse):
    fine, mid = [rhs_fine, beta_fine], [rhs_mid, beta_mid]
    blocks = pack_coarse(rhs_coarse, beta_coarse)
    z_first, z_last = pack_z(fine, mid)
    blocks, z_first, z_last = lax.optimization_barrier((blocks, z_first, z_last))
    z_next, z_prev = send(z_first, "gz", -1), send(z_last, "gz", 1)
    chips = [[2 * z + core for z in range(8)] for core in range(2)]
    blocks = jnp.broadcast_to(blocks, (8,) + blocks.shape)
    column = lax.all_to_all(blocks, "gz", 0, 0, axis_index_groups=chips)
    parts = gather(column, True)
    parts, z_next, z_prev = lax.optimization_barrier((parts, z_next, z_prev))
    zh, y_first, y_last = pack_y(fine, mid, z_next, z_prev)
    y_next, y_prev = send(y_first, "gy", -1), send(y_last, "gy", 1)
    parts = gather(join(parts, True).reshape((32, 4) + VREG), False)
    parts, y_next, y_prev = lax.optimization_barrier((parts, y_next, y_prev))
    own = join(parts, False)
    other = lax.ppermute(own, "gz", [(i, i ^ 1) for i in range(16)])
    down, up, down2, up2 = pack_x(fine, mid, zh, y_next, y_prev)
    x_next, x_prev = send(down, "gx", -1), send(up, "gx", 1)
    x_next2, x_prev2 = send(down2, "gx", -2), send(up2, "gx", 2)
    window = solve(own, other)
    return smooth(window, down, up, x_next, x_prev, x_next2, x_prev2)


def solution(mesh):
    spec = P("gx", "gy", "gz")
    return jax.shard_map(
        shards, mesh=mesh, in_specs=(spec,) * 6, out_specs=(spec, spec), check_vma=False
    )
```

```python
import jax
import jax.numpy as jnp
from jax import lax
from jax.experimental import pallas as pl
from jax.experimental.pallas import tpu as pltpu
from jax.sharding import PartitionSpec as P

ITERS = 8
SWEEPS = 2
F32 = jnp.float32
VREG = (8, 128)

NX, NJ, NK = 8, 4, 16
KC = 4

FY, FZ = 5, 5
MY, MZ = 4, 3
FT, MT = FY * FZ, MY * MZ
PAIRS = 8
F_SEND = 4 * 2 * FT
SEND = F_SEND + 4 * 2 * MT
Y_FINE = 2 * 4 * FZ
SHIFTS = (0, 1, 3, 2)


def iota(dim):
    return lax.broadcasted_iota(jnp.int32, VREG, dim)


def params(mib):
    return pltpu.CompilerParams(vmem_limit_bytes=mib * 2**20)


def tiles(n):
    return jax.ShapeDtypeStruct((n,) + VREG, F32)


def pack_kernel(*refs):
    ins, coarse, outs, blocks, scratch = refs[:8], refs[8:10], refs[10:12], refs[12], refs[13]
    lane = iota(1)
    for arr, ref in enumerate(coarse):
        for xi in range(2):
            gap = jnp.zeros((56, 128), F32)
            scratch[...] = jnp.concatenate([ref[xi], gap, pltpu.roll(ref[xi], 4, 0), gap], axis=0).T
            acc = jnp.zeros(VREG, F32)
            for zlo in range(16):
                rows = scratch[pl.ds(zlo, 8, stride=16), :]
                if zlo:
                    rows = pltpu.roll(rows, 4 * zlo, 1)
                acc = jnp.where(lane % 64 // 4 == zlo, rows, acc)
            for device in range(arr, 16, 2):
                blocks[device, xi] = acc
    for side in range(2):
        at = 0
        for ref in ins[side * 4 : side * 4 + 4]:
            planes, rows, _ = ref.shape
            for x in range(planes):
                for yt in range(rows // 8):
                    outs[side][at] = ref[x, yt * 8 : yt * 8 + 8, :]
                    at += 1


def pack(fine, mid, coarse):
    specs, args = [], []
    for last in (0, 1):
        for a in fine + mid:
            x, y, z = a.shape
            block = (z // 128 - 1) * last
            specs.append(pl.BlockSpec((x, y, 128), lambda i, block=block: (0, 0, block)))
            args.append(a)
    specs += [pl.BlockSpec((2,) + VREG, lambda i: (0, 0, 0))] * 2
    whole = pl.BlockSpec((80,) + VREG, lambda i: (0, 0, 0))
    return pl.pallas_call(
        pack_kernel,
        grid=(1,),
        in_specs=specs,
        out_specs=(whole, whole, pl.BlockSpec((16, 2) + VREG, lambda i: (0, 0, 0, 0))),
        out_shape=(tiles(80), tiles(80), jax.ShapeDtypeStruct((16, 2) + VREG, F32)),
        scratch_shapes=[pltpu.VMEM((128, 128), F32)],
        name="pack",
    )(*args, *coarse)


def pack_y_kernel(*refs):
    ins, (nxt, prv), (zh, first, last) = refs[:8], refs[8:10], refs[10:]
    right = iota(1) < 64
    for at in range(80):
        zh[at] = jnp.where(right, nxt[at], prv[at])
    below = iota(0) < 4
    for side, out in enumerate((first, last)):

        def tile(n, x, zt):
            ref = ins[side * 4 + n]
            if zt < ref.shape[2] // 128:
                return ref[x, :, zt * 128 : zt * 128 + 128]
            return zh[(n * 8 + x) * 4 + 3 * side] if n < 2 else zh[64 + ((n - 2) * 4 + x) * 2 + side]

        at = 0
        for n in range(2):
            for x in range(0, 8, 2):
                for zt in range(FZ):
                    one, two = tile(n, x, zt), pltpu.roll(tile(n, x + 1, zt), 4, 0)
                    out[at] = jnp.where(below, two, one) if side else jnp.where(below, one, two)
                    at += 1
        for n in range(2, 4):
            for x in range(4):
                for zt in range(MZ):
                    out[at] = tile(n, x, zt)
                    at += 1


def pack_y(fine, mid, nxt, prv):
    specs, args = [], []
    for last in (0, 1):
        for a in fine + mid:
            x, y, z = a.shape
            block = (y // 8 - 1) * last
            specs.append(pl.BlockSpec((x, 8, z), lambda i, block=block: (0, block, 0)))
            args.append(a)
    n = Y_FINE + 2 * 4 * MZ
    eighty = pl.BlockSpec((80,) + VREG, lambda i: (0, 0, 0))
    rows = pl.BlockSpec((n,) + VREG, lambda i: (0, 0, 0))
    return pl.pallas_call(
        pack_y_kernel,
        grid=(1,),
        in_specs=specs + [eighty, eighty],
        out_specs=(eighty, rows, rows),
        out_shape=(tiles(80), tiles(n), tiles(n)),
        name="pack_y",
    )(*args, nxt, prv)


def pack_x_kernel(rf, bf, rm, bm, zh, nxt, prv, down, up, across):
    below = iota(0) < 4
    low_half = lax.axis_index("gx") < 2

    def fine_plane(x, out, p):
        for a, ref in enumerate((rf, bf)):
            base = (p * 2 + a) * FT
            for yt in range(4):
                for zt in range(4):
                    out[base + yt * FZ + zt] = ref[x, yt * 8 : yt * 8 + 8, zt * 128 : zt * 128 + 128]
                out[base + yt * FZ + 4] = zh[(a * 8 + x) * 4 + yt]
            for zt in range(FZ):
                at = (a * 4 + x // 2) * FZ + zt
                if x % 2:
                    edge = pltpu.roll(jnp.where(below, prv[at], nxt[at]), 4, 0)
                else:
                    edge = jnp.where(below, nxt[at], prv[at])
                out[base + 4 * FZ + zt] = edge

    for p in range(4):
        fine_plane(p, down, p)
        fine_plane(p + 4, up, p)
        for a, ref in enumerate((rm, bm)):
            plane = []
            for yt in range(2):
                for zt in range(2):
                    plane.append(ref[p, yt * 8 : yt * 8 + 8, zt * 128 : zt * 128 + 128])
                plane.append(zh[64 + (a * 4 + p) * 2 + yt])
            for side in (nxt, prv):
                for zt in range(MZ):
                    plane.append(side[Y_FINE + (a * 4 + p) * MZ + zt])
            for i, tile in enumerate(plane):
                down[F_SEND + (p * 2 + a) * MT + i] = tile
                up[F_SEND + (p * 2 + a) * MT + i] = tile
                at = (p % 2 * 2 + a) * MT + i
                if p < 2:
                    across[at] = tile
                else:
                    across[at] = jnp.where(low_half, tile, across[at])


def pack_x(fine, mid, zh, nxt, prv):
    return pl.pallas_call(
        pack_x_kernel,
        out_shape=(tiles(SEND), tiles(SEND), tiles(4 * MT)),
        compiler_params=params(32),
        name="pack_x",
    )(*fine, *mid, zh, nxt, prv)


def column_kernel(blocks, out):
    for xi in range(2):
        rows = jnp.concatenate([blocks[z, xi] for z in range(16)], axis=0).T
        for h in range(2):
            for i in range(8):
                row = h * 64 + i * 8
                out[h * 16 + xi * 8 + i] = rows[row : row + 8]


def column(blocks):
    return pl.pallas_call(column_kernel, out_shape=tiles(32), name="column")(blocks)


def join_kernel(y_on_first_core, *refs):
    ins, out = refs[:4], refs[4]
    gx, gy, gz = lax.axis_index("gx"), lax.axis_index("gy"), lax.axis_index("gz")
    along_y = (lax.rem(gz, 2) == 0) == y_on_first_core
    mine = jnp.where(along_y, gy, gx)
    for step, ref in zip(SHIFTS, ins):
        slot = lax.rem(mine + 4 - step, 4)
        if len(out.shape) == 4:
            for i in range(32):
                out[slot, i] = ref[i]
        else:
            for other in range(4):
                x, y = jnp.where(along_y, other, slot), jnp.where(along_y, slot, other)
                for i in range(32):
                    out[x, y, i] = ref[other, i]


def join(parts, y_on_first_core):
    return pl.pallas_call(
        lambda *refs: join_kernel(y_on_first_core, *refs),
        out_shape=jax.ShapeDtypeStruct((4,) + parts[0].shape, F32),
        compiler_params=params(16),
        name="join",
    )(*parts)


def gather(part, y_on_first_core):
    def device(x, y, z):
        return (x % 4 * 4 + y % 4) * 16 + z

    parts = [part]
    for step in SHIFTS[1:]:
        pairs = []
        for x in range(4):
            for y in range(4):
                for z in range(16):
                    along_y = (z % 2 == 0) == y_on_first_core
                    to = device(x, y + step, z) if along_y else device(x + step, y, z)
                    pairs.append((device(x, y, z), to))
        parts.append(lax.ppermute(part, ("gx", "gy", "gz"), pairs))
    return parts


def solve_kernel(own, other, window, beta, rhat, r, v, t, x, vp, vs, wx, wy, wz, nat):
    gx, gy, gz = lax.axis_index("gx"), lax.axis_index("gy"), lax.axis_index("gz")
    lane, sub = iota(1), iota(0)
    first_core = lax.rem(gz, 2) == 0

    def unpack(rhs_ref, beta_ref):
        def body(bx, _):
            for xi in range(2):
                for k in range(NK):
                    for j in range(NJ):
                        rows = pl.ds(xi * 64 + k * 4 + j, 8, stride=128)
                        rhat[2 * bx + xi, j, k] = rhs_ref[bx, rows, :]
                        beta[2 * bx + xi, j, k] = 0.5 * beta_ref[bx, rows, :]
            return 0

        lax.fori_loop(0, 4, body, 0)

    @pl.when(first_core)
    def _():
        unpack(own, other)

    @pl.when(jnp.logical_not(first_core))
    def _():
        unpack(other, own)

    def shift_up(a):
        return jnp.where(sub == 0, 0.0, pltpu.roll(a, 1, 0))

    def shift_down(a):
        return jnp.where(sub == 7, 0.0, pltpu.roll(a, 7, 0))

    def shift_right(a):
        return jnp.where(lane == 0, 0.0, pltpu.roll(a, 1, 1))

    def shift_left(a):
        return jnp.where(lane == 127, 0.0, pltpu.roll(a, 127, 1))

    wx[0] = beta[0]
    wx[NX] = beta[NX - 1]

    def faces(xx, _):
        @pl.when(xx > 0)
        def _():
            for j in range(NJ):
                for k in range(NK):
                    wx[xx, j, k] = beta[xx - 1, j, k] + beta[xx, j, k]

        for k in range(NK):
            col = [beta[xx, j, k] for j in range(NJ)]
            col = [shift_up(col[3])] + col + [shift_down(col[0])]
            for j in range(NJ + 1):
                wy[xx, j, k] = col[j] + col[j + 1]
        for j in range(NJ):
            row = [beta[xx, j, k] for k in range(NK)]
            row = [shift_right(row[15])] + row + [shift_left(row[0])]
            for k in range(NK + 1):
                wz[xx, j, k] = row[k] + row[k + 1]
        return 0

    lax.fori_loop(0, NX, faces, 0)

    def put(vec, xx, j, k, value):
        vec[xx + 1, j, k + 1] = value
        if k == 0:
            vec[xx + 1, j, NK + 1] = shift_left(value)
        if k == NK - 1:
            vec[xx + 1, j, 0] = shift_right(value)

    def total(acc):
        out = acc[0]
        for a in acc[1:]:
            out = out + a
        for k in (4, 2, 1):
            out = out + pltpu.roll(out, k, 0)
        return jnp.broadcast_to(jnp.sum(out, axis=1, keepdims=True), VREG)

    CELLS = [(j, k) for j in range(NJ) for k in range(KC)]

    def operate(vec, out, sums):
        def body(i, acc):
            k0 = i * KC
            acc = list(acc)
            centre = {c: vec[1, c[0], k0 + 1 + c[1]] for c in CELLS}
            low = {c: wx[0, c[0], k0 + c[1]] * centre[c] for c in CELLS}
            for xx in range(NX):
                if xx + 1 < NX:
                    after = {c: vec[xx + 2, c[0], k0 + 1 + c[1]] for c in CELLS}
                    high = {c: wx[xx + 1, c[0], k0 + c[1]] * (after[c] - centre[c]) for c in CELLS}
                else:
                    after = None
                    high = {c: -(wx[xx + 1, c[0], k0 + c[1]] * centre[c]) for c in CELLS}
                value = {c: low[c] - high[c] for c in CELLS}
                for k in range(KC):
                    col = [centre[j, k] for j in range(NJ)]
                    col = [shift_up(col[3])] + col + [shift_down(col[0])]
                    flux = [wy[xx, j, k0 + k] * (col[j + 1] - col[j]) for j in range(NJ + 1)]
                    for j in range(NJ):
                        value[j, k] = value[j, k] + (flux[j] - flux[j + 1])
                for j in range(NJ):
                    row = [vec[xx + 1, j, k0]] + [centre[j, k] for k in range(KC)] + [vec[xx + 1, j, k0 + KC + 1]]
                    flux = [wz[xx, j, k0 + k] * (row[k + 1] - row[k]) for k in range(KC + 1)]
                    for k in range(KC):
                        value[j, k] = value[j, k] + (flux[k] - flux[k + 1])
                for c in CELLS:
                    out[xx, c[0], k0 + c[1]] = value[c]
                    terms = sums(value[c], centre[c], rhat[xx, c[0], k0 + c[1]])
                    slot = c[1]
                    for n, term in enumerate(terms):
                        acc[n * KC + slot] = acc[n * KC + slot] + term
                centre, low = after, high
            return tuple(acc)

        zero = jnp.zeros(VREG, F32)
        n = len(sums(zero, zero, zero))
        acc = lax.fori_loop(0, NK // KC, body, (zero,) * (n * KC))
        return [total(acc[m * KC : m * KC + KC]) for m in range(n)]

    def start(xx, acc):
        for j in range(NJ):
            for k in range(NK):
                a = rhat[xx, j, k]
                r[xx, j, k] = a
                x[xx, j, k] = jnp.zeros(VREG, F32)
                put(vp, xx, j, k, a)
                acc = acc + a * a
        return acc

    rho = total([lax.fori_loop(0, NX, start, jnp.zeros(VREG, F32))])

    def iteration(step, rho, last=False):
        (rv,) = operate(vp, v, lambda av, _, rh: (rh * av,))
        alpha = rho / rv

        def half(xx, _):
            for j in range(NJ):
                for k in range(NK):
                    put(vs, xx, j, k, r[xx, j, k] - alpha * v[xx, j, k])
            return 0

        lax.fori_loop(0, NX, half, 0, unroll=4)
        ts, tt, rt = operate(vs, t, lambda at, s, rh: (at * s, at * at, rh * at))
        omega = ts / tt
        rho_new = -omega * rt
        scale = rho_new / rho * (alpha / omega)

        def update(xx, _):
            for j in range(NJ):
                for k in range(NK):
                    p, s = vp[xx + 1, j, k + 1], vs[xx + 1, j, k + 1]
                    x[xx, j, k] = x[xx, j, k] + (alpha * p + omega * s)
                    if not last:
                        res = s - omega * t[xx, j, k]
                        r[xx, j, k] = res
                        put(vp, xx, j, k, res + scale * (p - omega * v[xx, j, k]))
            return 0

        lax.fori_loop(0, NX, update, 0, unroll=4)
        return rho_new

    rho = lax.fori_loop(0, ITERS - 1, iteration, rho)
    iteration(ITERS - 1, rho, True)

    first = lax.rem(128 + 8 * gz - 2, 128)

    def extract(i, _):
        xx = jnp.clip(2 * gx - 3 + i, 0, NX - 1)
        for h in range(2):
            nat[h, 0:8, :] = jnp.zeros(VREG, F32)
            nat[h, 40:48, :] = jnp.zeros(VREG, F32)
            for j in range(NJ):
                acc = jnp.zeros(VREG, F32)
                for kk in range(8):
                    rolled = pltpu.roll(x[xx, j, h * 8 + kk], lax.rem(16 * kk + 128 - first, 128), 1)
                    acc = jnp.where(lane // 16 == kk, rolled, acc)
                nat[h, pl.ds(8 + j, 8, stride=4), :] = acc
            for tile, row in enumerate((8 * gy + 8, 8 * gy + 16, 8 * gy)):
                window[i, tile, h] = nat[h, pl.ds(pl.multiple_of(row, 8), 8), :]
        return 0

    lax.fori_loop(0, 8, extract, 0)


def solve(own, other):
    full = pltpu.VMEM((NX, NJ, NK) + VREG, F32)
    vector = pltpu.VMEM((NX + 2, NJ, NK + 2) + VREG, F32)
    return pl.pallas_call(
        solve_kernel,
        out_shape=jax.ShapeDtypeStruct((8, 3, 2) + VREG, F32),
        scratch_shapes=[full] * 6
        + [
            vector,
            vector,
            pltpu.VMEM((NX + 1, NJ, NK) + VREG, F32),
            pltpu.VMEM((NX, NJ + 1, NK) + VREG, F32),
            pltpu.VMEM((NX, NJ, NK + 1) + VREG, F32),
            pltpu.VMEM((2, 48, 128), F32),
        ],
        compiler_params=params(34),
        cost_estimate=pl.CostEstimate(flops=400_000_000, bytes_accessed=100_000_000, transcendentals=0),
        name="solve",
    )(own.reshape(4, 1024, 128), other.reshape(4, 1024, 128))


def level_helpers(ny, nz):
    lane, sub = iota(1), iota(0)

    def up_rolled(row):
        return [pltpu.roll(p, 1, 0) for p in row]

    def down_rolled(row):
        return [pltpu.roll(p, 7, 0) for p in row]

    def from_above(edge, here):
        return [jnp.where(sub == 0, p, q) for p, q in zip(edge, here)]

    def from_below(edge, here):
        return [jnp.where(sub == 7, p, q) for p, q in zip(edge, here)]

    def from_left(row):
        rolled = [pltpu.roll(p, 1, 1) for p in row]
        return [jnp.where(lane == 0, rolled[b - 1], rolled[b]) for b in range(nz)]

    def from_right(row):
        rolled = [pltpu.roll(p, 127, 1) for p in row]
        return [jnp.where(lane == 127, rolled[(b + 1) % nz], rolled[b]) for b in range(nz)]

    def load(ref, m, a):
        return [ref[m, (a % ny) * nz + b] for b in range(nz)]

    return up_rolled, down_rolled, from_above, from_below, from_left, from_right, load


def prepare_level(w, ny, nz, inside):
    up_rolled, down_rolled, from_above, from_below, from_left, from_right, load = level_helpers(ny, nz)
    even = lax.rem(iota(0) + iota(1), 2) == 0

    def body(m, _):
        before, after = jnp.maximum(m - 1, 0), jnp.minimum(m + 1, PAIRS - 1)
        last = [up_rolled(load(w.b[c], m, ny - 1)) for c in (0, 1)]
        first = waiting = None

        def finish(a, diag, here, edge):
            for c in (0, 1):
                high = from_below(edge[1 - c], here[1 - c])
                for b in range(nz):
                    i = a * nz + b
                    w.inv[c][m, i] = jnp.where(inside(m, i), 1.0 / (diag[c][b] + high[b]), 0.0)

        for a in range(ny):
            rows = [load(w.b[c], m, a) for c in (0, 1)]
            rolled = [up_rolled(rows[c]) for c in (0, 1)]
            low_y = [[p + q for p, q in zip(rows[c], from_above(last[1 - c], rolled[1 - c]))] for c in (0, 1)]
            last = rolled
            low_z = [[p + q for p, q in zip(rows[c], from_left(rows[1 - c]))] for c in (0, 1)]
            diag = []
            for c in (0, 1):
                high_z = from_right(low_z[1 - c])
                total = []
                for b in range(nz):
                    i = a * nz + b
                    x_in = rows[0][b] + rows[1][b]
                    lower, upper = w.b[1 - c][before, i], w.b[1 - c][after, i]
                    x_out = rows[c][b] + (jnp.where(even, lower, upper) if c == 0 else jnp.where(even, upper, lower))
                    if c == 0:
                        w.x_in[m, i] = x_in
                    w.x_out[c][m, i] = x_out
                    w.y[c][m, i] = low_y[c][b]
                    w.z[c][m, i] = low_z[c][b]
                    total.append((x_in + x_out) + low_y[c][b] + (low_z[c][b] + high_z[b]))
                diag.append(total)
            here = [down_rolled(low_y[c]) for c in (0, 1)]
            if a == 0:
                first = here
            else:
                finish(a - 1, waiting[0], waiting[1], here)
            waiting = (diag, here)
        finish(ny - 1, waiting[0], waiting[1], first)
        return 0

    lax.fori_loop(0, PAIRS, body, 0)


def smooth_level(w, ny, nz):
    up_rolled, down_rolled, from_above, from_below, from_left, from_right, load = level_helpers(ny, nz)
    even = lax.rem(iota(0) + iota(1), 2) == 0

    for half in range(2 * SWEEPS):
        c = half % 2
        old, new = w.e[1 - c], w.e[c]

        def body(m, _, c=c, old=old, new=new):
            before, after = jnp.maximum(m - 1, 0), jnp.minimum(m + 1, PAIRS - 1)

            def lowered(a, row):
                return down_rolled([p * q for p, q in zip(load(w.y[1 - c], m, a), row)])

            last = up_rolled(load(old, m, ny - 1))
            row = load(old, m, 0)
            here = first = lowered(0, row)
            for a in range(ny):
                rolled = up_rolled(row)
                up = from_above(last, rolled)
                if a + 1 < ny:
                    row_next = load(old, m, a + 1)
                    edge = lowered(a + 1, row_next)
                else:
                    row_next, edge = None, first
                down = from_below(edge, here)
                left = from_left(row)
                right = from_right([p * q for p, q in zip(load(w.z[1 - c], m, a), row)])
                for b in range(nz):
                    i = a * nz + b
                    lower, upper = old[before, i], old[after, i]
                    far = jnp.where(even, lower, upper) if c == 0 else jnp.where(even, upper, lower)
                    off = w.x_in[m, i] * row[b] + w.x_out[c][m, i] * far
                    off = off + (w.y[c][m, i] * up[b] + down[b]) + (w.z[c][m, i] * left[b] + right[b])
                    new[m, i] = (w.r[c][m, i] + off) * w.inv[c][m, i]
                last, row, here = rolled, row_next, edge
            return 0

        skip = (half + 1) // 2
        lax.fori_loop(skip, PAIRS - skip, body, 0)


class Level:
    def __init__(self, refs):
        refs = list(refs)
        self.x_in = refs[0]
        self.e, self.r, self.b, self.x_out, self.y, self.z, self.inv = (refs[1 + 2 * i : 3 + 2 * i] for i in range(7))


def smooth_kernel(window, down, up, nxt, prv, far, out_fine, out_coarse, *scratch):
    gx, gy, gz = lax.axis_index("gx"), lax.axis_index("gy"), lax.axis_index("gz")
    lane, sub = iota(1), iota(0)
    even = lax.rem(lane + sub, 2) == 0
    mid, fine = Level(scratch[:15]), Level(scratch[15:])

    def place(ref, base, n, level, pair0, pairs, half=0.5):
        def copy(p, _):
            at = base + p * 4 * n
            for i in range(n):
                for kind, dest, scale in ((0, level.r, None), (1, level.b, half)):
                    one, two = ref[at + kind * n + i], ref[at + 2 * n + kind * n + i]
                    if scale is not None:
                        one, two = scale * one, scale * two
                    dest[0][pair0 + p, i] = jnp.where(even, one, two)
                    dest[1][pair0 + p, i] = jnp.where(even, two, one)
            return 0

        lax.fori_loop(0, pairs, copy, 0)

    place(far, 0, MT, mid, 0, 1, jnp.where(gx >= 2, 0.5, 0.0))
    place(prv, F_SEND, MT, mid, 1, 2)
    place(down, F_SEND, MT, mid, 3, 2)
    place(nxt, F_SEND, MT, mid, 5, 2)
    place(far, 0, MT, mid, 7, 1, jnp.where(gx < 2, 0.5, 0.0))
    place(prv, 0, FT, fine, 0, 2)
    place(down, 0, FT, fine, 2, 2)
    place(up, 0, FT, fine, 4, 2)
    place(nxt, 0, FT, fine, 6, 2)

    everywhere = jnp.full(VREG, True)
    in_z = ((lane < 64) & (gz < 15)) | ((lane >= 64) & (gz > 0))
    in_y = ((sub < 4) & (gy < 3)) | ((sub >= 4) & (gy > 0))

    def inside_x(m, first, size):
        return (2 * m + first >= 0) & (2 * m + first < size)

    def mid_inside(m, i):
        yt, zt = i // MZ, i % MZ
        y = everywhere if yt < 2 else jnp.full(VREG, gy < 3 if yt == 2 else gy > 0)
        return y & (everywhere if zt < 2 else in_z) & inside_x(m, 4 * gx - 6, 16)

    def fine_inside(m, i):
        yt, zt = i // FZ, i % FZ
        return (in_y if yt == 4 else everywhere) & (in_z if zt == 4 else everywhere) & inside_x(m, 8 * gx - 4, 32)

    prepare_level(mid, MY, MZ, mid_inside)
    prepare_level(fine, FY, FZ, fine_inside)

    src = lax.broadcasted_iota(jnp.int32, (256, 512), 0)
    dst = lax.broadcasted_iota(jnp.int32, (256, 512), 1)
    cell = 16 * (src % 16 - 2) + src // 16
    lanes = jnp.where(dst >= 320, dst - 384, dst)
    wanted = jnp.where(dst >= 384, dst - 384, (lanes + 128) // 2 - 64)
    pick = (cell == wanted).astype(F32)
    source = jnp.concatenate(
        [
            jnp.concatenate([window[i, tile, 0], window[i, tile, 1]], axis=1)
            for i in range(8)
            for tile in range(3)
        ],
        axis=0,
    )
    wide = jnp.dot(source, pick, precision=lax.Precision.HIGHEST, preferred_element_type=F32)

    def tile_of(i, tile, zt):
        row = (i * 3 + tile) * 8
        return wide[row : row + 8, zt * 128 : zt * 128 + 128]

    for i in range(2):
        out_coarse[i] = tile_of(3 + i, 0, 3)

    def doubled_rows(a, half):
        return jnp.take_along_axis(a, sub // 2 + 4 * half, axis=0, mode="promise_in_bounds")

    def doubled_lanes(a, half):
        return jnp.take_along_axis(a, lane // 2 + 64 * half, axis=1, mode="promise_in_bounds")

    for i in range(8):
        for zt in range(MZ):
            plane = [
                doubled_rows(tile_of(i, 0, zt), 0),
                doubled_rows(tile_of(i, 0, zt), 1),
                doubled_rows(tile_of(i, 1, zt), 0),
                doubled_rows(tile_of(i, 2, zt), 1),
            ]
            for yt in range(MY):
                mid.e[1][i, yt * MZ + zt] = jnp.where(mid_inside(i, yt * MZ + zt), plane[yt], 0.0)

    smooth_level(mid, MY, MZ)

    def prolong(pair, _):
        for odd in range(2):
            plane = []
            for b in range(MZ):
                src = []
                for a in range(MY):
                    red, black = (mid.e[c][pair + 2, a * MZ + b] for c in (0, 1))
                    src.append(jnp.where(even, black, red) if odd else jnp.where(even, red, black))
                edge = jnp.where(sub < 4, doubled_rows(src[2], 0), doubled_rows(src[3], 1))
                plane.append([doubled_rows(src[a // 2], a % 2) for a in range(4)] + [edge])
            for a in range(FY):
                row = [doubled_lanes(plane[b // 2][a], b % 2) for b in range(4)]
                last = plane[2][a]
                row.append(jnp.where(lane < 64, doubled_lanes(last, 0), doubled_lanes(last, 1)))
                for b in range(FZ):
                    fine.e[1][2 * pair + odd, a * FZ + b] = row[b]
        return 0

    lax.fori_loop(0, 4, prolong, 0)
    smooth_level(fine, FY, FZ)

    def store(p, _):
        for a in range(4):
            for b in range(4):
                red, black = (fine.e[c][p + 2, a * FZ + b] for c in (0, 1))
                out_fine[2 * p, a * 8 : a * 8 + 8, b * 128 : b * 128 + 128] = jnp.where(even, red, black)
                out_fine[2 * p + 1, a * 8 : a * 8 + 8, b * 128 : b * 128 + 128] = jnp.where(even, black, red)
        return 0

    lax.fori_loop(0, 4, store, 0)


def smooth(window, *parts):
    mid = pltpu.VMEM((PAIRS, MT) + VREG, F32)
    fine = pltpu.VMEM((PAIRS, FT) + VREG, F32)
    return pl.pallas_call(
        smooth_kernel,
        out_shape=(jax.ShapeDtypeStruct((8, 32, 512), F32), jax.ShapeDtypeStruct((2,) + VREG, F32)),
        scratch_shapes=[mid] * 15 + [fine] * 15,
        compiler_params=params(48),
        name="smooth",
    )(window, *parts)


def send(a, axis, step):
    n = lax.axis_size(axis)
    return lax.ppermute(a, axis, [(i, i + step) for i in range(n) if 0 <= i + step < n])


def shards(rhs_fine, beta_fine, rhs_mid, beta_mid, rhs_coarse, beta_coarse):
    fine, mid = [rhs_fine, beta_fine], [rhs_mid, beta_mid]
    z_first, z_last, blocks = pack(fine, mid, [rhs_coarse, beta_coarse])
    z_next, z_prev = send(z_first, "gz", -1), send(z_last, "gz", 1)
    col = column(lax.all_to_all(blocks, "gz", 0, 0))
    col, z_next, z_prev = lax.optimization_barrier((col, z_next, z_prev))
    parts = gather(col, True)
    zh, y_first, y_last = pack_y(fine, mid, z_next, z_prev)
    parts, y_first, y_last = lax.optimization_barrier((parts, y_first, y_last))
    y_next, y_prev = send(y_first, "gy", -1), send(y_last, "gy", 1)
    parts = gather(join(parts, True), False)
    parts, y_next, y_prev = lax.optimization_barrier((parts, y_next, y_prev))
    own = join(parts, False)
    other = lax.ppermute(own, "gz", [(i, i ^ 1) for i in range(16)])
    down, up, across = pack_x(fine, mid, zh, y_next, y_prev)
    x_next, x_prev = send(down, "gx", -1), send(up, "gx", 1)
    x_far = lax.ppermute(across, "gx", [(i, (i + 2) % 4) for i in range(4)])
    window = solve(own, other)
    return smooth(window, down, up, x_next, x_prev, x_far)


def solution(mesh):
    spec = P("gx", "gy", "gz")
    return jax.shard_map(
        shards, mesh=mesh, in_specs=(spec,) * 6, out_specs=(spec, spec), check_vma=False
    )
```

```python
import jax
import jax.numpy as jnp
from jax import lax
from jax.experimental import pallas as pl
from jax.experimental.pallas import tpu as pltpu
from jax.sharding import PartitionSpec as P

ITERS = 8
SWEEPS = 2
F32 = jnp.float32
VREG = (8, 128)

NX, NJ, NK = 8, 4, 16
KC = 4

FY, FZ = 5, 5
MY, MZ = 4, 3
FT, MT = FY * FZ, MY * MZ
PAIRS = 8
F_SEND = 4 * 2 * FT
SEND = F_SEND + 4 * 2 * MT
Y_FINE = 2 * 4 * 4
Y_SEND = Y_FINE + 2 * 4 * 2
YH = 2 * 8 * 4
Z_MID = 2 * 8 * FY
Z_SEND = Z_MID + 2 * 4 * MY
SHIFTS = (0, 1, 3, 2)
HALF = 132
COLUMN = 2 * HALF // 8


def iota(dim):
    return lax.broadcasted_iota(jnp.int32, VREG, dim)


def params(mib):
    return pltpu.CompilerParams(vmem_limit_bytes=mib * 2**20)


def tiles(n):
    return jax.ShapeDtypeStruct((n,) + VREG, F32)


def pack_coarse_kernel(rhs, beta, blocks, scratch):
    lane = iota(1)
    for arr, ref in enumerate((rhs, beta)):
        for xi in range(2):
            gap = jnp.zeros((56, 128), F32)
            scratch[...] = jnp.concatenate([ref[xi], gap, pltpu.roll(ref[xi], 4, 0), gap], axis=0).T
            acc = jnp.zeros(VREG, F32)
            for zlo in range(16):
                rows = scratch[pl.ds(zlo, 8, stride=16), :]
                if zlo:
                    rows = pltpu.roll(rows, 4 * zlo, 1)
                acc = jnp.where(lane % 64 // 4 == zlo, rows, acc)
            for device in range(arr, 16, 2):
                blocks[device, xi] = acc


def pack_coarse(rhs, beta):
    return pl.pallas_call(
        pack_coarse_kernel,
        out_shape=jax.ShapeDtypeStruct((16, 2) + VREG, F32),
        scratch_shapes=[pltpu.VMEM((128, 128), F32)],
        name="pack_coarse",
    )(rhs, beta)


def pack_y_kernel(*refs):
    ins, outs = refs[:8], refs[8:]
    below = iota(0) < 4
    for side, out in enumerate(outs):

        def tile(n, x, zt):
            return ins[side * 4 + n][x, :, zt * 128 : zt * 128 + 128]

        at = 0
        for n in range(2):
            for x in range(0, 8, 2):
                for zt in range(4):
                    one, two = tile(n, x, zt), pltpu.roll(tile(n, x + 1, zt), 4, 0)
                    out[at] = jnp.where(below, two, one) if side else jnp.where(below, one, two)
                    at += 1
        for n in range(2, 4):
            for x in range(4):
                for zt in range(2):
                    out[at] = tile(n, x, zt)
                    at += 1


def edges(arrays, dim):
    specs = []
    for last in (0, 1):
        for a in arrays:
            shape, index = list(a.shape), [0, 0, 0]
            size = (8, 128)[dim - 1]
            index[dim] = (shape[dim] // size - 1) * last
            shape[dim] = size
            specs.append(pl.BlockSpec(tuple(shape), lambda i, index=tuple(index): index))
    return specs, list(arrays) * 2


def whole(shape):
    return pl.BlockSpec(shape, lambda i: (0,) * len(shape))


def pack_y(fine, mid):
    specs, args = edges(fine + mid, 1)
    rows = (Y_SEND,) + VREG
    return pl.pallas_call(
        pack_y_kernel,
        grid=(1,),
        in_specs=specs,
        out_specs=(whole(rows), whole(rows)),
        out_shape=(tiles(Y_SEND), tiles(Y_SEND)),
        name="pack_y",
    )(*args)


def pack_z_kernel(*refs):
    ins, (nxt, prv), (yh, first, last) = refs[:8], refs[8:10], refs[10:]
    below = iota(0) < 4
    for n in range(2):
        for x in range(8):
            for zt in range(4):
                at = (n * 4 + x // 2) * 4 + zt
                if x % 2:
                    tile = pltpu.roll(jnp.where(below, prv[at], nxt[at]), 4, 0)
                else:
                    tile = jnp.where(below, nxt[at], prv[at])
                yh[(n * 8 + x) * 4 + zt] = tile
    for at in range(16):
        yh[YH + at] = nxt[Y_FINE + at]
        yh[YH + 16 + at] = prv[Y_FINE + at]
    for side, out in enumerate((first, last)):
        at = 0
        for n in range(4):
            ref = ins[side * 4 + n]
            planes, rows, _ = ref.shape
            for x in range(planes):
                for yt in range(rows // 8):
                    out[at] = ref[x, yt * 8 : yt * 8 + 8, :]
                    at += 1
                if n < 2:
                    out[at] = yh[(n * 8 + x) * 4 + 3 * side]
                    at += 1
                else:
                    for way in range(2):
                        out[at] = yh[YH + 16 * way + ((n - 2) * 4 + x) * 2 + side]
                        at += 1


def pack_z(fine, mid, nxt, prv):
    specs, args = edges(fine + mid, 2)
    rows, merged, lanes = (Y_SEND,) + VREG, (YH + 32,) + VREG, (Z_SEND,) + VREG
    return pl.pallas_call(
        pack_z_kernel,
        grid=(1,),
        in_specs=specs + [whole(rows)] * 2,
        out_specs=(whole(merged), whole(lanes), whole(lanes)),
        out_shape=(tiles(YH + 32), tiles(Z_SEND), tiles(Z_SEND)),
        compiler_params=params(12),
        name="pack_z",
    )(*args, nxt, prv)


def pack_x_kernel(rf, bf, rm, bm, yh, nxt, prv, down, up, across):
    right = iota(1) < 64
    low_half = lax.axis_index("gx") < 2

    def merged(at):
        return jnp.where(right, nxt[at], prv[at])

    def fine_plane(x, out, p):
        for a, ref in enumerate((rf, bf)):
            base = (p * 2 + a) * FT
            for yt in range(FY):
                for zt in range(4):
                    if yt < 4:
                        tile = ref[x, yt * 8 : yt * 8 + 8, zt * 128 : zt * 128 + 128]
                    else:
                        tile = yh[(a * 8 + x) * 4 + zt]
                    out[base + yt * FZ + zt] = tile
                out[base + yt * FZ + 4] = merged((a * 8 + x) * FY + yt)

    for p in range(4):
        fine_plane(p, down, p)
        fine_plane(p + 4, up, p)
        for a, ref in enumerate((rm, bm)):
            plane = []
            for yt in range(MY):
                for zt in range(2):
                    if yt < 2:
                        plane.append(ref[p, yt * 8 : yt * 8 + 8, zt * 128 : zt * 128 + 128])
                    else:
                        plane.append(yh[YH + 16 * (yt - 2) + (a * 4 + p) * 2 + zt])
                plane.append(merged(Z_MID + (a * 4 + p) * MY + yt))
            for i, tile in enumerate(plane):
                down[F_SEND + (p * 2 + a) * MT + i] = tile
                up[F_SEND + (p * 2 + a) * MT + i] = tile
                at = (p % 2 * 2 + a) * MT + i
                if p < 2:
                    across[at] = tile
                else:
                    across[at] = jnp.where(low_half, tile, across[at])


def pack_x(fine, mid, yh, nxt, prv):
    return pl.pallas_call(
        pack_x_kernel,
        out_shape=(tiles(SEND), tiles(SEND), tiles(4 * MT)),
        compiler_params=params(32),
        name="pack_x",
    )(*fine, *mid, yh, nxt, prv)


def column_kernel(blocks, out):
    out[HALF - 4 : HALF, :] = jnp.zeros((4, 128), F32)
    out[2 * HALF - 4 : 2 * HALF, :] = jnp.zeros((4, 128), F32)
    for xi in range(2):
        rows = jnp.concatenate([blocks[z, xi] for z in range(16)], axis=0).T
        for h in range(2):
            at = h * HALF + xi * 64
            out[at : at + 64, :] = rows[h * 64 : h * 64 + 64]


def column(blocks):
    out = pl.pallas_call(
        column_kernel,
        out_shape=jax.ShapeDtypeStruct((2 * HALF, 128), F32),
        compiler_params=params(12),
        name="column",
    )(blocks)
    return out.reshape((COLUMN,) + VREG)


def join_kernel(y_on_first_core, *refs):
    ins, out = refs[:4], refs[4]
    gx, gy, gz = lax.axis_index("gx"), lax.axis_index("gy"), lax.axis_index("gz")
    along_y = (lax.rem(gz, 2) == 0) == y_on_first_core
    mine = jnp.where(along_y, gy, gx)
    for step, ref in zip(SHIFTS, ins):
        slot = lax.rem(mine + 4 - step, 4)
        if len(out.shape) == 4:
            for i in range(COLUMN):
                out[slot, i] = ref[i]
        else:
            for other in range(4):
                x, y = jnp.where(along_y, other, slot), jnp.where(along_y, slot, other)
                for i in range(COLUMN):
                    out[x, y, i] = ref[other, i]


def join(parts, y_on_first_core):
    return pl.pallas_call(
        lambda *refs: join_kernel(y_on_first_core, *refs),
        out_shape=jax.ShapeDtypeStruct((4,) + parts[0].shape, F32),
        compiler_params=params(16),
        name="join",
    )(*parts)


def gather(part, y_on_first_core):
    def device(x, y, z):
        return (x % 4 * 4 + y % 4) * 16 + z

    parts = [part]
    for step in SHIFTS[1:]:
        pairs = []
        for x in range(4):
            for y in range(4):
                for z in range(16):
                    along_y = (z % 2 == 0) == y_on_first_core
                    to = device(x, y + step, z) if along_y else device(x + step, y, z)
                    pairs.append((device(x, y, z), to))
        parts.append(lax.ppermute(part, ("gx", "gy", "gz"), pairs))
    return parts


def solve_kernel(own, other, window, beta, rhat, r, v, t, x, vp, vs, wx, wy, wz, nat):
    gx, gy, gz = lax.axis_index("gx"), lax.axis_index("gy"), lax.axis_index("gz")
    lane, sub = iota(1), iota(0)
    first_core = lax.rem(gz, 2) == 0

    def unpack(rhs_ref, beta_ref):
        def body(bx, _):
            for xi in range(2):
                for k in range(NK):
                    for j in range(NJ):
                        rows = pl.ds(xi * 64 + k * 4 + j, 8, stride=HALF)
                        rhat[2 * bx + xi, j, k] = rhs_ref[bx, rows, :]
                        beta[2 * bx + xi, j, k] = 0.5 * beta_ref[bx, rows, :]
            return 0

        lax.fori_loop(0, 4, body, 0)

    @pl.when(first_core)
    def _():
        unpack(own, other)

    @pl.when(jnp.logical_not(first_core))
    def _():
        unpack(other, own)

    def shift_up(a):
        return jnp.where(sub == 0, 0.0, pltpu.roll(a, 1, 0))

    def shift_down(a):
        return jnp.where(sub == 7, 0.0, pltpu.roll(a, 7, 0))

    def shift_right(a):
        return jnp.where(lane == 0, 0.0, pltpu.roll(a, 1, 1))

    def shift_left(a):
        return jnp.where(lane == 127, 0.0, pltpu.roll(a, 127, 1))

    wx[0] = beta[0]
    wx[NX] = beta[NX - 1]

    def faces(xx, _):
        @pl.when(xx > 0)
        def _():
            for j in range(NJ):
                for k in range(NK):
                    wx[xx, j, k] = beta[xx - 1, j, k] + beta[xx, j, k]

        for k in range(NK):
            col = [beta[xx, j, k] for j in range(NJ)]
            col = [shift_up(col[3])] + col + [shift_down(col[0])]
            for j in range(NJ + 1):
                wy[xx, j, k] = col[j] + col[j + 1]
        for j in range(NJ):
            row = [beta[xx, j, k] for k in range(NK)]
            row = [shift_right(row[15])] + row + [shift_left(row[0])]
            for k in range(NK + 1):
                wz[xx, j, k] = row[k] + row[k + 1]
        return 0

    lax.fori_loop(0, NX, faces, 0, unroll=2)

    def put(vec, xx, j, k, value):
        vec[xx + 1, j, k + 1] = value
        if k == 0:
            vec[xx + 1, j, NK + 1] = shift_left(value)
        if k == NK - 1:
            vec[xx + 1, j, 0] = shift_right(value)

    def total(acc):
        out = acc[0]
        for a in acc[1:]:
            out = out + a
        for k in (4, 2, 1):
            out = out + pltpu.roll(out, k, 0)
        return jnp.broadcast_to(jnp.sum(out, axis=1, keepdims=True), VREG)

    CELLS = [(j, k) for j in range(NJ) for k in range(KC)]

    def operate(vec, out, sums):
        def body(i, acc):
            k0 = i * KC
            acc = list(acc)
            centre = {c: vec[1, c[0], k0 + 1 + c[1]] for c in CELLS}
            low = {c: wx[0, c[0], k0 + c[1]] * centre[c] for c in CELLS}
            for xx in range(NX):
                if xx + 1 < NX:
                    after = {c: vec[xx + 2, c[0], k0 + 1 + c[1]] for c in CELLS}
                    high = {c: wx[xx + 1, c[0], k0 + c[1]] * (after[c] - centre[c]) for c in CELLS}
                else:
                    after = None
                    high = {c: -(wx[xx + 1, c[0], k0 + c[1]] * centre[c]) for c in CELLS}
                value = {c: low[c] - high[c] for c in CELLS}
                for k in range(KC):
                    col = [centre[j, k] for j in range(NJ)]
                    col = [shift_up(col[3])] + col + [shift_down(col[0])]
                    flux = [wy[xx, j, k0 + k] * (col[j + 1] - col[j]) for j in range(NJ + 1)]
                    for j in range(NJ):
                        value[j, k] = value[j, k] + (flux[j] - flux[j + 1])
                for j in range(NJ):
                    row = [vec[xx + 1, j, k0]] + [centre[j, k] for k in range(KC)] + [vec[xx + 1, j, k0 + KC + 1]]
                    flux = [wz[xx, j, k0 + k] * (row[k + 1] - row[k]) for k in range(KC + 1)]
                    for k in range(KC):
                        value[j, k] = value[j, k] + (flux[k] - flux[k + 1])
                for c in CELLS:
                    out[xx, c[0], k0 + c[1]] = value[c]
                    terms = sums(value[c], centre[c], rhat[xx, c[0], k0 + c[1]])
                    slot = c[1]
                    for n, term in enumerate(terms):
                        acc[n * KC + slot] = acc[n * KC + slot] + term
                centre, low = after, high
            return tuple(acc)

        zero = jnp.zeros(VREG, F32)
        n = len(sums(zero, zero, zero))
        acc = lax.fori_loop(0, NK // KC, body, (zero,) * (n * KC))
        return [total(acc[m * KC : m * KC + KC]) for m in range(n)]

    def start(xx, acc):
        for j in range(NJ):
            for k in range(NK):
                a = rhat[xx, j, k]
                r[xx, j, k] = a
                x[xx, j, k] = jnp.zeros(VREG, F32)
                put(vp, xx, j, k, a)
                acc = acc + a * a
        return acc

    rho = total([lax.fori_loop(0, NX, start, jnp.zeros(VREG, F32))])

    def iteration(step, rho, last=False):
        (rv,) = operate(vp, v, lambda av, _, rh: (rh * av,))
        alpha = rho / rv

        def half(xx, _):
            for j in range(NJ):
                for k in range(NK):
                    put(vs, xx, j, k, r[xx, j, k] - alpha * v[xx, j, k])
            return 0

        lax.fori_loop(0, NX, half, 0, unroll=4)
        ts, tt, rt = operate(vs, t, lambda at, s, rh: (at * s, at * at, rh * at))
        omega = ts / tt
        rho_new = -omega * rt
        scale = rho_new / rho * (alpha / omega)

        def update(xx, _):
            for j in range(NJ):
                for k in range(NK):
                    p, s = vp[xx + 1, j, k + 1], vs[xx + 1, j, k + 1]
                    x[xx, j, k] = x[xx, j, k] + (alpha * p + omega * s)
                    if not last:
                        res = s - omega * t[xx, j, k]
                        r[xx, j, k] = res
                        put(vp, xx, j, k, res + scale * (p - omega * v[xx, j, k]))
            return 0

        lax.fori_loop(0, NX, update, 0, unroll=4)
        return rho_new

    rho = lax.fori_loop(0, ITERS - 1, iteration, rho)
    iteration(ITERS - 1, rho, True)

    first = lax.rem(128 + 8 * gz - 2, 128)

    def extract(i, _):
        xx = jnp.clip(2 * gx - 3 + i, 0, NX - 1)
        for h in range(2):
            nat[h, 0:8, :] = jnp.zeros(VREG, F32)
            nat[h, 40:48, :] = jnp.zeros(VREG, F32)
            for j in range(NJ):
                acc = jnp.zeros(VREG, F32)
                for kk in range(8):
                    rolled = pltpu.roll(x[xx, j, h * 8 + kk], lax.rem(16 * kk + 128 - first, 128), 1)
                    acc = jnp.where(lane // 16 == kk, rolled, acc)
                nat[h, pl.ds(8 + j, 8, stride=4), :] = acc
            for tile, row in enumerate((8 * gy + 8, 8 * gy + 16, 8 * gy)):
                window[i, tile, h] = nat[h, pl.ds(pl.multiple_of(row, 8), 8), :]
        return 0

    lax.fori_loop(0, 8, extract, 0, unroll=4)


def solve(own, other):
    full = pltpu.VMEM((NX, NJ, NK) + VREG, F32)
    vector = pltpu.VMEM((NX + 2, NJ, NK + 2) + VREG, F32)
    return pl.pallas_call(
        solve_kernel,
        out_shape=jax.ShapeDtypeStruct((8, 3, 2) + VREG, F32),
        scratch_shapes=[full] * 6
        + [
            vector,
            vector,
            pltpu.VMEM((NX + 1, NJ, NK) + VREG, F32),
            pltpu.VMEM((NX, NJ + 1, NK) + VREG, F32),
            pltpu.VMEM((NX, NJ, NK + 1) + VREG, F32),
            pltpu.VMEM((2, 48, 128), F32),
        ],
        compiler_params=params(34),
        cost_estimate=pl.CostEstimate(flops=400_000_000, bytes_accessed=100_000_000, transcendentals=0),
        name="solve",
    )(own.reshape(4, 8 * HALF, 128), other.reshape(4, 8 * HALF, 128))


def level_helpers(ny, nz):
    lane, sub = iota(1), iota(0)

    def up_rolled(row):
        return [pltpu.roll(p, 1, 0) for p in row]

    def down_rolled(row):
        return [pltpu.roll(p, 7, 0) for p in row]

    def from_above(edge, here):
        return [jnp.where(sub == 0, p, q) for p, q in zip(edge, here)]

    def from_below(edge, here):
        return [jnp.where(sub == 7, p, q) for p, q in zip(edge, here)]

    def from_left(row):
        rolled = [pltpu.roll(p, 1, 1) for p in row]
        return [jnp.where(lane == 0, rolled[b - 1], rolled[b]) for b in range(nz)]

    def from_right(row):
        rolled = [pltpu.roll(p, 127, 1) for p in row]
        return [jnp.where(lane == 127, rolled[(b + 1) % nz], rolled[b]) for b in range(nz)]

    def load(ref, m, a):
        return [ref[m, (a % ny) * nz + b] for b in range(nz)]

    return up_rolled, down_rolled, from_above, from_below, from_left, from_right, load


def prepare_level(w, ny, nz, inside):
    up_rolled, down_rolled, from_above, from_below, from_left, from_right, load = level_helpers(ny, nz)
    even = lax.rem(iota(0) + iota(1), 2) == 0

    def body(m, _):
        before, after = jnp.maximum(m - 1, 0), jnp.minimum(m + 1, PAIRS - 1)
        last = [up_rolled(load(w.b[c], m, ny - 1)) for c in (0, 1)]
        first = waiting = None

        def finish(a, diag, here, edge):
            for c in (0, 1):
                high = from_below(edge[1 - c], here[1 - c])
                for b in range(nz):
                    i = a * nz + b
                    w.inv[c][m, i] = jnp.where(inside(m, i), 1.0 / (diag[c][b] + high[b]), 0.0)

        for a in range(ny):
            rows = [load(w.b[c], m, a) for c in (0, 1)]
            rolled = [up_rolled(rows[c]) for c in (0, 1)]
            low_y = [[p + q for p, q in zip(rows[c], from_above(last[1 - c], rolled[1 - c]))] for c in (0, 1)]
            last = rolled
            low_z = [[p + q for p, q in zip(rows[c], from_left(rows[1 - c]))] for c in (0, 1)]
            diag = []
            for c in (0, 1):
                high_z = from_right(low_z[1 - c])
                total = []
                for b in range(nz):
                    i = a * nz + b
                    x_in = rows[0][b] + rows[1][b]
                    lower, upper = w.b[1 - c][before, i], w.b[1 - c][after, i]
                    x_out = rows[c][b] + (jnp.where(even, lower, upper) if c == 0 else jnp.where(even, upper, lower))
                    if c == 0:
                        w.x_in[m, i] = x_in
                    w.x_out[c][m, i] = x_out
                    w.y[c][m, i] = low_y[c][b]
                    w.z[c][m, i] = low_z[c][b]
                    total.append((x_in + x_out) + low_y[c][b] + (low_z[c][b] + high_z[b]))
                diag.append(total)
            here = [down_rolled(low_y[c]) for c in (0, 1)]
            if a == 0:
                first = here
            else:
                finish(a - 1, waiting[0], waiting[1], here)
            waiting = (diag, here)
        finish(ny - 1, waiting[0], waiting[1], first)
        return 0

    lax.fori_loop(0, PAIRS, body, 0, unroll=2)


def smooth_level(w, ny, nz):
    up_rolled, down_rolled, from_above, from_below, from_left, from_right, load = level_helpers(ny, nz)
    even = lax.rem(iota(0) + iota(1), 2) == 0

    for half in range(2 * SWEEPS):
        c = half % 2
        old, new = w.e[1 - c], w.e[c]

        def body(m, _, c=c, old=old, new=new):
            before, after = jnp.maximum(m - 1, 0), jnp.minimum(m + 1, PAIRS - 1)

            def lowered(a, row):
                return down_rolled([p * q for p, q in zip(load(w.y[1 - c], m, a), row)])

            last = up_rolled(load(old, m, ny - 1))
            row = load(old, m, 0)
            here = first = lowered(0, row)
            for a in range(ny):
                rolled = up_rolled(row)
                up = from_above(last, rolled)
                if a + 1 < ny:
                    row_next = load(old, m, a + 1)
                    edge = lowered(a + 1, row_next)
                else:
                    row_next, edge = None, first
                down = from_below(edge, here)
                left = from_left(row)
                right = from_right([p * q for p, q in zip(load(w.z[1 - c], m, a), row)])
                for b in range(nz):
                    i = a * nz + b
                    lower, upper = old[before, i], old[after, i]
                    far = jnp.where(even, lower, upper) if c == 0 else jnp.where(even, upper, lower)
                    off = w.x_in[m, i] * row[b] + w.x_out[c][m, i] * far
                    off = off + (w.y[c][m, i] * up[b] + down[b]) + (w.z[c][m, i] * left[b] + right[b])
                    new[m, i] = (w.r[c][m, i] + off) * w.inv[c][m, i]
                last, row, here = rolled, row_next, edge
            return 0

        skip = (half + 1) // 2
        lax.fori_loop(skip, PAIRS - skip, body, 0, unroll=4)


class Level:
    def __init__(self, refs):
        refs = list(refs)
        self.x_in = refs[0]
        self.e, self.r, self.b, self.x_out, self.y, self.z, self.inv = (refs[1 + 2 * i : 3 + 2 * i] for i in range(7))


def smooth_kernel(window, down, up, nxt, prv, far, out_fine, out_coarse, *scratch):
    gx, gy, gz = lax.axis_index("gx"), lax.axis_index("gy"), lax.axis_index("gz")
    lane, sub = iota(1), iota(0)
    even = lax.rem(lane + sub, 2) == 0
    mid, fine = Level(scratch[:15]), Level(scratch[15:])

    def place(ref, base, n, level, pair0, pairs, half=0.5):
        def copy(p, _):
            at = base + p * 4 * n
            for i in range(n):
                for kind, dest, scale in ((0, level.r, None), (1, level.b, half)):
                    one, two = ref[at + kind * n + i], ref[at + 2 * n + kind * n + i]
                    if scale is not None:
                        one, two = scale * one, scale * two
                    dest[0][pair0 + p, i] = jnp.where(even, one, two)
                    dest[1][pair0 + p, i] = jnp.where(even, two, one)
            return 0

        lax.fori_loop(0, pairs, copy, 0)

    place(far, 0, MT, mid, 0, 1, jnp.where(gx >= 2, 0.5, 0.0))
    place(prv, F_SEND, MT, mid, 1, 2)
    place(down, F_SEND, MT, mid, 3, 2)
    place(nxt, F_SEND, MT, mid, 5, 2)
    place(far, 0, MT, mid, 7, 1, jnp.where(gx < 2, 0.5, 0.0))
    place(prv, 0, FT, fine, 0, 2)
    place(down, 0, FT, fine, 2, 2)
    place(up, 0, FT, fine, 4, 2)
    place(nxt, 0, FT, fine, 6, 2)

    everywhere = jnp.full(VREG, True)
    in_z = ((lane < 64) & (gz < 15)) | ((lane >= 64) & (gz > 0))
    in_y = ((sub < 4) & (gy < 3)) | ((sub >= 4) & (gy > 0))

    def inside_x(m, first, size):
        return (2 * m + first >= 0) & (2 * m + first < size)

    def mid_inside(m, i):
        yt, zt = i // MZ, i % MZ
        y = everywhere if yt < 2 else jnp.full(VREG, gy < 3 if yt == 2 else gy > 0)
        return y & (everywhere if zt < 2 else in_z) & inside_x(m, 4 * gx - 6, 16)

    def fine_inside(m, i):
        yt, zt = i // FZ, i % FZ
        return (in_y if yt == 4 else everywhere) & (in_z if zt == 4 else everywhere) & inside_x(m, 8 * gx - 4, 32)

    prepare_level(mid, MY, MZ, mid_inside)
    prepare_level(fine, FY, FZ, fine_inside)

    src = lax.broadcasted_iota(jnp.int32, (256, 512), 0)
    dst = lax.broadcasted_iota(jnp.int32, (256, 512), 1)
    cell = 16 * (src % 16 - 2) + src // 16
    lanes = jnp.where(dst >= 320, dst - 384, dst)
    wanted = jnp.where(dst >= 384, dst - 384, (lanes + 128) // 2 - 64)
    pick = (cell == wanted).astype(F32)
    source = jnp.concatenate(
        [
            jnp.concatenate([window[i, tile, 0], window[i, tile, 1]], axis=1)
            for i in range(8)
            for tile in range(3)
        ],
        axis=0,
    )
    wide = jnp.dot(source, pick, precision=lax.Precision.HIGHEST, preferred_element_type=F32)

    def tile_of(i, tile, zt):
        row = (i * 3 + tile) * 8
        return wide[row : row + 8, zt * 128 : zt * 128 + 128]

    for i in range(2):
        out_coarse[i] = tile_of(3 + i, 0, 3)

    def doubled_rows(a, half):
        return jnp.take_along_axis(a, sub // 2 + 4 * half, axis=0, mode="promise_in_bounds")

    def doubled_lanes(a, half):
        return jnp.take_along_axis(a, lane // 2 + 64 * half, axis=1, mode="promise_in_bounds")

    for i in range(8):
        for zt in range(MZ):
            plane = [
                doubled_rows(tile_of(i, 0, zt), 0),
                doubled_rows(tile_of(i, 0, zt), 1),
                doubled_rows(tile_of(i, 1, zt), 0),
                doubled_rows(tile_of(i, 2, zt), 1),
            ]
            for yt in range(MY):
                mid.e[1][i, yt * MZ + zt] = jnp.where(mid_inside(i, yt * MZ + zt), plane[yt], 0.0)

    smooth_level(mid, MY, MZ)

    def prolong(pair, _):
        for odd in range(2):
            plane = []
            for b in range(MZ):
                src = []
                for a in range(MY):
                    red, black = (mid.e[c][pair + 2, a * MZ + b] for c in (0, 1))
                    src.append(jnp.where(even, black, red) if odd else jnp.where(even, red, black))
                edge = jnp.where(sub < 4, doubled_rows(src[2], 0), doubled_rows(src[3], 1))
                plane.append([doubled_rows(src[a // 2], a % 2) for a in range(4)] + [edge])
            for a in range(FY):
                row = [doubled_lanes(plane[b // 2][a], b % 2) for b in range(4)]
                last = plane[2][a]
                row.append(jnp.where(lane < 64, doubled_lanes(last, 0), doubled_lanes(last, 1)))
                for b in range(FZ):
                    fine.e[1][2 * pair + odd, a * FZ + b] = row[b]
        return 0

    lax.fori_loop(0, 4, prolong, 0)
    smooth_level(fine, FY, FZ)

    def store(p, _):
        for a in range(4):
            for b in range(4):
                red, black = (fine.e[c][p + 2, a * FZ + b] for c in (0, 1))
                out_fine[2 * p, a * 8 : a * 8 + 8, b * 128 : b * 128 + 128] = jnp.where(even, red, black)
                out_fine[2 * p + 1, a * 8 : a * 8 + 8, b * 128 : b * 128 + 128] = jnp.where(even, black, red)
        return 0

    lax.fori_loop(0, 4, store, 0)


def smooth(window, *parts):
    mid = pltpu.VMEM((PAIRS, MT) + VREG, F32)
    fine = pltpu.VMEM((PAIRS, FT) + VREG, F32)
    return pl.pallas_call(
        smooth_kernel,
        out_shape=(jax.ShapeDtypeStruct((8, 32, 512), F32), jax.ShapeDtypeStruct((2,) + VREG, F32)),
        scratch_shapes=[mid] * 15 + [fine] * 15,
        compiler_params=params(48),
        name="smooth",
    )(window, *parts)


def send(a, axis, step):
    n = lax.axis_size(axis)
    return lax.ppermute(a, axis, [(i, i + step) for i in range(n) if 0 <= i + step < n])


def shards(rhs_fine, beta_fine, rhs_mid, beta_mid, rhs_coarse, beta_coarse):
    fine, mid = [rhs_fine, beta_fine], [rhs_mid, beta_mid]
    blocks = pack_coarse(rhs_coarse, beta_coarse)
    y_first, y_last = pack_y(fine, mid)
    y_next, y_prev = send(y_first, "gy", -1), send(y_last, "gy", 1)
    col = column(lax.all_to_all(blocks, "gz", 0, 0))
    parts = gather(col, True)
    yh, z_first, z_last = pack_z(fine, mid, y_next, y_prev)
    parts, z_first, z_last = lax.optimization_barrier((parts, z_first, z_last))
    z_next, z_prev = send(z_first, "gz", -1), send(z_last, "gz", 1)
    parts = gather(join(parts, True), False)
    parts, z_next, z_prev = lax.optimization_barrier((parts, z_next, z_prev))
    own = join(parts, False)
    other = lax.ppermute(own, "gz", [(i, i ^ 1) for i in range(16)])
    down, up, across = pack_x(fine, mid, yh, z_next, z_prev)
    x_next, x_prev = send(down, "gx", -1), send(up, "gx", 1)
    x_far = lax.ppermute(across, "gx", [(i, (i + 2) % 4) for i in range(4)])
    window = solve(own, other)
    return smooth(window, down, up, x_next, x_prev, x_far)


def solution(mesh):
    spec = P("gx", "gy", "gz")
    return jax.shard_map(
        shards, mesh=mesh, in_specs=(spec,) * 6, out_specs=(spec, spec), check_vma=False
    )
```

```python
import jax
import jax.numpy as jnp
from jax import lax
from jax.experimental import pallas as pl
from jax.experimental.pallas import tpu as pltpu
from jax.sharding import PartitionSpec as P

ITERS = 8
SWEEPS = 2
F32 = jnp.float32
VREG = (8, 128)

NX, NJ, NK = 8, 4, 16
KC = 4

FY, FZ = 5, 5
MY, MZ = 4, 3
FT, MT = FY * FZ, MY * MZ
PAIRS = 8
F_SEND = 4 * 2 * FT
SEND = F_SEND + 4 * 2 * MT
Y_FINE = 2 * 4 * 4
Y_SEND = Y_FINE + 2 * 4 * 2
YH = 2 * 8 * 4
Z_MID = 2 * 8 * FY
Z_SEND = Z_MID + 2 * 4 * MY
SHIFTS = (0, 1, 3, 2)
HALF = 132
COLUMN = 2 * HALF // 8


def iota(dim):
    return lax.broadcasted_iota(jnp.int32, VREG, dim)


def params(mib):
    return pltpu.CompilerParams(vmem_limit_bytes=mib * 2**20)


def tiles(n):
    return jax.ShapeDtypeStruct((n,) + VREG, F32)


def pack_kernel(*refs):
    ins, coarse, outs, blocks, scratch = refs[:8], refs[8:10], refs[10:12], refs[12], refs[13]
    lane = iota(1)
    for arr, ref in enumerate(coarse):
        for xi in range(2):
            gap = jnp.zeros((56, 128), F32)
            scratch[...] = jnp.concatenate([ref[xi], gap, pltpu.roll(ref[xi], 4, 0), gap], axis=0).T
            acc = jnp.zeros(VREG, F32)
            for zlo in range(16):
                rows = scratch[pl.ds(zlo, 8, stride=16), :]
                if zlo:
                    rows = pltpu.roll(rows, 4 * zlo, 1)
                acc = jnp.where(lane % 64 // 4 == zlo, rows, acc)
            for device in range(arr, 16, 2):
                blocks[device, xi] = acc
    below = iota(0) < 4
    for side, out in enumerate(outs):

        def tile(n, x, zt):
            return ins[side * 4 + n][x, :, zt * 128 : zt * 128 + 128]

        at = 0
        for n in range(2):
            for x in range(0, 8, 2):
                for zt in range(4):
                    one, two = tile(n, x, zt), pltpu.roll(tile(n, x + 1, zt), 4, 0)
                    out[at] = jnp.where(below, two, one) if side else jnp.where(below, one, two)
                    at += 1
        for n in range(2, 4):
            for x in range(4):
                for zt in range(2):
                    out[at] = tile(n, x, zt)
                    at += 1


def edges(arrays, dim):
    specs = []
    for last in (0, 1):
        for a in arrays:
            shape, index = list(a.shape), [0, 0, 0]
            size = (8, 128)[dim - 1]
            index[dim] = (shape[dim] // size - 1) * last
            shape[dim] = size
            specs.append(pl.BlockSpec(tuple(shape), lambda i, index=tuple(index): index))
    return specs, list(arrays) * 2


def whole(shape):
    return pl.BlockSpec(shape, lambda i: (0,) * len(shape))


def pack(fine, mid, coarse):
    specs, args = edges(fine + mid, 1)
    rows, blocks = (Y_SEND,) + VREG, (16, 2) + VREG
    return pl.pallas_call(
        pack_kernel,
        grid=(1,),
        in_specs=specs + [whole((2,) + VREG)] * 2,
        out_specs=(whole(rows), whole(rows), whole(blocks)),
        out_shape=(tiles(Y_SEND), tiles(Y_SEND), jax.ShapeDtypeStruct(blocks, F32)),
        scratch_shapes=[pltpu.VMEM((128, 128), F32)],
        name="pack",
    )(*args, *coarse)


def pack_z_kernel(*refs):
    ins, (nxt, prv), (yh, first, last) = refs[:8], refs[8:10], refs[10:]
    below = iota(0) < 4
    for n in range(2):
        for x in range(8):
            for zt in range(4):
                at = (n * 4 + x // 2) * 4 + zt
                if x % 2:
                    tile = pltpu.roll(jnp.where(below, prv[at], nxt[at]), 4, 0)
                else:
                    tile = jnp.where(below, nxt[at], prv[at])
                yh[(n * 8 + x) * 4 + zt] = tile
    for at in range(16):
        yh[YH + at] = nxt[Y_FINE + at]
        yh[YH + 16 + at] = prv[Y_FINE + at]
    for side, out in enumerate((first, last)):
        at = 0
        for n in range(4):
            ref = ins[side * 4 + n]
            planes, rows, _ = ref.shape
            for x in range(planes):
                for yt in range(rows // 8):
                    out[at] = ref[x, yt * 8 : yt * 8 + 8, :]
                    at += 1
                if n < 2:
                    out[at] = yh[(n * 8 + x) * 4 + 3 * side]
                    at += 1
                else:
                    for way in range(2):
                        out[at] = yh[YH + 16 * way + ((n - 2) * 4 + x) * 2 + side]
                        at += 1


def pack_z(fine, mid, nxt, prv):
    specs, args = edges(fine + mid, 2)
    rows, merged, lanes = (Y_SEND,) + VREG, (YH + 32,) + VREG, (Z_SEND,) + VREG
    return pl.pallas_call(
        pack_z_kernel,
        grid=(1,),
        in_specs=specs + [whole(rows)] * 2,
        out_specs=(whole(merged), whole(lanes), whole(lanes)),
        out_shape=(tiles(YH + 32), tiles(Z_SEND), tiles(Z_SEND)),
        compiler_params=params(12),
        name="pack_z",
    )(*args, nxt, prv)


def pack_x_kernel(rf, bf, rm, bm, yh, nxt, prv, down, up, across):
    right = iota(1) < 64
    low_half = lax.axis_index("gx") < 2

    def merged(at):
        return jnp.where(right, nxt[at], prv[at])

    def fine_plane(x, out, p):
        for a, ref in enumerate((rf, bf)):
            base = (p * 2 + a) * FT
            for yt in range(FY):
                for zt in range(4):
                    if yt < 4:
                        tile = ref[x, yt * 8 : yt * 8 + 8, zt * 128 : zt * 128 + 128]
                    else:
                        tile = yh[(a * 8 + x) * 4 + zt]
                    out[base + yt * FZ + zt] = tile
                out[base + yt * FZ + 4] = merged((a * 8 + x) * FY + yt)

    for p in range(4):
        fine_plane(p, down, p)
        fine_plane(p + 4, up, p)
        for a, ref in enumerate((rm, bm)):
            plane = []
            for yt in range(MY):
                for zt in range(2):
                    if yt < 2:
                        plane.append(ref[p, yt * 8 : yt * 8 + 8, zt * 128 : zt * 128 + 128])
                    else:
                        plane.append(yh[YH + 16 * (yt - 2) + (a * 4 + p) * 2 + zt])
                plane.append(merged(Z_MID + (a * 4 + p) * MY + yt))
            for i, tile in enumerate(plane):
                down[F_SEND + (p * 2 + a) * MT + i] = tile
                up[F_SEND + (p * 2 + a) * MT + i] = tile
                at = (p % 2 * 2 + a) * MT + i
                if p < 2:
                    across[at] = tile
                else:
                    across[at] = jnp.where(low_half, tile, across[at])


def pack_x(fine, mid, yh, nxt, prv):
    return pl.pallas_call(
        pack_x_kernel,
        out_shape=(tiles(SEND), tiles(SEND), tiles(4 * MT)),
        compiler_params=params(32),
        name="pack_x",
    )(*fine, *mid, yh, nxt, prv)


def column_kernel(blocks, out):
    out[HALF - 4 : HALF, :] = jnp.zeros((4, 128), F32)
    out[2 * HALF - 4 : 2 * HALF, :] = jnp.zeros((4, 128), F32)
    for xi in range(2):
        rows = jnp.concatenate([blocks[z, xi] for z in range(16)], axis=0).T
        for h in range(2):
            at = h * HALF + xi * 64
            out[at : at + 64, :] = rows[h * 64 : h * 64 + 64]


def column(blocks):
    out = pl.pallas_call(
        column_kernel,
        out_shape=jax.ShapeDtypeStruct((2 * HALF, 128), F32),
        compiler_params=params(12),
        name="column",
    )(blocks)
    return out.reshape((COLUMN,) + VREG)


def join_kernel(y_on_first_core, *refs):
    ins, out = refs[:4], refs[4]
    gx, gy, gz = lax.axis_index("gx"), lax.axis_index("gy"), lax.axis_index("gz")
    along_y = (lax.rem(gz, 2) == 0) == y_on_first_core
    mine = jnp.where(along_y, gy, gx)
    for step, ref in zip(SHIFTS, ins):
        slot = lax.rem(mine + 4 - step, 4)
        if len(out.shape) == 4:
            for i in range(COLUMN):
                out[slot, i] = ref[i]
        else:
            for other in range(4):
                x, y = jnp.where(along_y, other, slot), jnp.where(along_y, slot, other)
                for i in range(COLUMN):
                    out[x, y, i] = ref[other, i]


def join(parts, y_on_first_core):
    return pl.pallas_call(
        lambda *refs: join_kernel(y_on_first_core, *refs),
        out_shape=jax.ShapeDtypeStruct((4,) + parts[0].shape, F32),
        compiler_params=params(16),
        name="join",
    )(*parts)


def gather(part, y_on_first_core):
    def device(x, y, z):
        return (x % 4 * 4 + y % 4) * 16 + z

    parts = [part]
    for step in SHIFTS[1:]:
        pairs = []
        for x in range(4):
            for y in range(4):
                for z in range(16):
                    along_y = (z % 2 == 0) == y_on_first_core
                    to = device(x, y + step, z) if along_y else device(x + step, y, z)
                    pairs.append((device(x, y, z), to))
        parts.append(lax.ppermute(part, ("gx", "gy", "gz"), pairs))
    return parts


def solve_kernel(own, other, window, beta, rhat, r, v, t, x, vp, vs, wx, wy, wz, nat):
    gx, gy, gz = lax.axis_index("gx"), lax.axis_index("gy"), lax.axis_index("gz")
    lane, sub = iota(1), iota(0)
    first_core = lax.rem(gz, 2) == 0

    def unpack(rhs_ref, beta_ref):
        def body(bx, _):
            for xi in range(2):
                for k in range(NK):
                    for j in range(NJ):
                        rows = pl.ds(xi * 64 + k * 4 + j, 8, stride=HALF)
                        rhat[2 * bx + xi, j, k] = rhs_ref[bx, rows, :]
                        beta[2 * bx + xi, j, k] = 0.5 * beta_ref[bx, rows, :]
            return 0

        lax.fori_loop(0, 4, body, 0, unroll=2)

    @pl.when(first_core)
    def _():
        unpack(own, other)

    @pl.when(jnp.logical_not(first_core))
    def _():
        unpack(other, own)

    def shift_up(a):
        return jnp.where(sub == 0, 0.0, pltpu.roll(a, 1, 0))

    def shift_down(a):
        return jnp.where(sub == 7, 0.0, pltpu.roll(a, 7, 0))

    def shift_right(a):
        return jnp.where(lane == 0, 0.0, pltpu.roll(a, 1, 1))

    def shift_left(a):
        return jnp.where(lane == 127, 0.0, pltpu.roll(a, 127, 1))

    wx[0] = beta[0]
    wx[NX] = beta[NX - 1]

    def faces(xx, _):
        @pl.when(xx > 0)
        def _():
            for j in range(NJ):
                for k in range(NK):
                    wx[xx, j, k] = beta[xx - 1, j, k] + beta[xx, j, k]

        for k in range(NK):
            col = [beta[xx, j, k] for j in range(NJ)]
            col = [shift_up(col[3])] + col + [shift_down(col[0])]
            for j in range(NJ):
                wy[xx, j, k] = col[j] + col[j + 1]
            wy[xx, NJ, k] = -col[NJ]
        for j in range(NJ):
            row = [beta[xx, j, k] for k in range(NK)]
            row = [shift_right(row[15])] + row + [shift_left(row[0])]
            for k in range(NK + 1):
                wz[xx, j, k] = row[k] + row[k + 1]
        return 0

    lax.fori_loop(0, NX, faces, 0, unroll=2)

    def put(vec, xx, j, k, value):
        vec[xx + 1, j, k + 1] = value
        if k == 0:
            vec[xx + 1, j, NK + 1] = shift_left(value)
        if k == NK - 1:
            vec[xx + 1, j, 0] = shift_right(value)

    def total(acc):
        out = acc[0]
        for a in acc[1:]:
            out = out + a
        for k in (4, 2, 1):
            out = out + pltpu.roll(out, k, 0)
        return jnp.broadcast_to(jnp.sum(out, axis=1, keepdims=True), VREG)

    CELLS = [(j, k) for j in range(NJ) for k in range(KC)]

    def operate(vec, out, sums):
        def body(i, acc):
            k0 = i * KC
            acc = list(acc)
            centre = {c: vec[1, c[0], k0 + 1 + c[1]] for c in CELLS}
            low = {c: wx[0, c[0], k0 + c[1]] * centre[c] for c in CELLS}
            for xx in range(NX):
                if xx + 1 < NX:
                    after = {c: vec[xx + 2, c[0], k0 + 1 + c[1]] for c in CELLS}
                    high = {c: wx[xx + 1, c[0], k0 + c[1]] * (after[c] - centre[c]) for c in CELLS}
                else:
                    after = None
                    high = {c: -(wx[xx + 1, c[0], k0 + c[1]] * centre[c]) for c in CELLS}
                value = {c: low[c] - high[c] for c in CELLS}
                for k in range(KC):
                    col = [centre[j, k] for j in range(NJ)]
                    col = [shift_up(col[3])] + col
                    flux = [wy[xx, j, k0 + k] * (col[j + 1] - col[j]) for j in range(NJ)]
                    flux.append(jnp.where(sub == 7, wy[xx, NJ, k0 + k] * col[NJ], pltpu.roll(flux[0], 7, 0)))
                    for j in range(NJ):
                        value[j, k] = value[j, k] + (flux[j] - flux[j + 1])
                for j in range(NJ):
                    row = [vec[xx + 1, j, k0]] + [centre[j, k] for k in range(KC)] + [vec[xx + 1, j, k0 + KC + 1]]
                    flux = [wz[xx, j, k0 + k] * (row[k + 1] - row[k]) for k in range(KC + 1)]
                    for k in range(KC):
                        value[j, k] = value[j, k] + (flux[k] - flux[k + 1])
                for c in CELLS:
                    out[xx, c[0], k0 + c[1]] = value[c]
                    terms = sums(value[c], centre[c], rhat[xx, c[0], k0 + c[1]])
                    slot = c[1]
                    for n, term in enumerate(terms):
                        acc[n * KC + slot] = acc[n * KC + slot] + term
                centre, low = after, high
            return tuple(acc)

        zero = jnp.zeros(VREG, F32)
        n = len(sums(zero, zero, zero))
        acc = lax.fori_loop(0, NK // KC, body, (zero,) * (n * KC), unroll=2)
        return [total(acc[m * KC : m * KC + KC]) for m in range(n)]

    def start(xx, acc):
        for j in range(NJ):
            for k in range(NK):
                a = rhat[xx, j, k]
                r[xx, j, k] = a
                x[xx, j, k] = jnp.zeros(VREG, F32)
                put(vp, xx, j, k, a)
                acc = acc + a * a
        return acc

    rho = total([lax.fori_loop(0, NX, start, jnp.zeros(VREG, F32))])

    def iteration(step, rho, last=False):
        (rv,) = operate(vp, v, lambda av, _, rh: (rh * av,))
        alpha = rho / rv

        def half(xx, _):
            for j in range(NJ):
                for k in range(NK):
                    put(vs, xx, j, k, r[xx, j, k] - alpha * v[xx, j, k])
            return 0

        lax.fori_loop(0, NX, half, 0, unroll=4)
        ts, tt, rt = operate(vs, t, lambda at, s, rh: (at * s, at * at, rh * at))
        omega = ts / tt
        rho_new = -omega * rt
        scale = rho_new / rho * (alpha / omega)

        def update(xx, _):
            for j in range(NJ):
                for k in range(NK):
                    p, s = vp[xx + 1, j, k + 1], vs[xx + 1, j, k + 1]
                    x[xx, j, k] = x[xx, j, k] + (alpha * p + omega * s)
                    if not last:
                        res = s - omega * t[xx, j, k]
                        r[xx, j, k] = res
                        put(vp, xx, j, k, res + scale * (p - omega * v[xx, j, k]))
            return 0

        lax.fori_loop(0, NX, update, 0, unroll=4)
        return rho_new

    rho = lax.fori_loop(0, ITERS - 1, iteration, rho)
    iteration(ITERS - 1, rho, True)

    first = lax.rem(128 + 8 * gz - 2, 128)

    def extract(i, _):
        xx = jnp.clip(2 * gx - 3 + i, 0, NX - 1)
        for h in range(2):
            nat[h, 0:8, :] = jnp.zeros(VREG, F32)
            nat[h, 40:48, :] = jnp.zeros(VREG, F32)
            for j in range(NJ):
                acc = jnp.zeros(VREG, F32)
                for kk in range(8):
                    rolled = pltpu.roll(x[xx, j, h * 8 + kk], lax.rem(16 * kk + 128 - first, 128), 1)
                    acc = jnp.where(lane // 16 == kk, rolled, acc)
                nat[h, pl.ds(8 + j, 8, stride=4), :] = acc
            for tile, row in enumerate((8 * gy + 8, 8 * gy + 16, 8 * gy)):
                window[i, tile, h] = nat[h, pl.ds(pl.multiple_of(row, 8), 8), :]
        return 0

    lax.fori_loop(0, 8, extract, 0, unroll=4)


def solve(own, other):
    full = pltpu.VMEM((NX, NJ, NK) + VREG, F32)
    vector = pltpu.VMEM((NX + 2, NJ, NK + 2) + VREG, F32)
    return pl.pallas_call(
        solve_kernel,
        out_shape=jax.ShapeDtypeStruct((8, 3, 2) + VREG, F32),
        scratch_shapes=[full] * 6
        + [
            vector,
            vector,
            pltpu.VMEM((NX + 1, NJ, NK) + VREG, F32),
            pltpu.VMEM((NX, NJ + 1, NK) + VREG, F32),
            pltpu.VMEM((NX, NJ, NK + 1) + VREG, F32),
            pltpu.VMEM((2, 48, 128), F32),
        ],
        compiler_params=params(34),
        cost_estimate=pl.CostEstimate(flops=400_000_000, bytes_accessed=100_000_000, transcendentals=0),
        name="solve",
    )(own.reshape(4, 8 * HALF, 128), other.reshape(4, 8 * HALF, 128))


def level_helpers(ny, nz):
    lane, sub = iota(1), iota(0)

    def up_rolled(row):
        return [pltpu.roll(p, 1, 0) for p in row]

    def down_rolled(row):
        return [pltpu.roll(p, 7, 0) for p in row]

    def from_above(edge, here):
        return [jnp.where(sub == 0, p, q) for p, q in zip(edge, here)]

    def from_below(edge, here):
        return [jnp.where(sub == 7, p, q) for p, q in zip(edge, here)]

    def from_left(row):
        rolled = [pltpu.roll(p, 1, 1) for p in row]
        return [jnp.where(lane == 0, rolled[b - 1], rolled[b]) for b in range(nz)]

    def from_right(row):
        rolled = [pltpu.roll(p, 127, 1) for p in row]
        return [jnp.where(lane == 127, rolled[(b + 1) % nz], rolled[b]) for b in range(nz)]

    def load(ref, m, a):
        return [ref[m, (a % ny) * nz + b] for b in range(nz)]

    return up_rolled, down_rolled, from_above, from_below, from_left, from_right, load


def prepare_level(w, ny, nz, inside):
    up_rolled, down_rolled, from_above, from_below, from_left, from_right, load = level_helpers(ny, nz)
    even = lax.rem(iota(0) + iota(1), 2) == 0

    def body(m, _):
        before, after = jnp.maximum(m - 1, 0), jnp.minimum(m + 1, PAIRS - 1)
        last = [up_rolled(load(w.b[c], m, ny - 1)) for c in (0, 1)]
        first = waiting = None

        def finish(a, diag, here, edge):
            for c in (0, 1):
                high = from_below(edge[1 - c], here[1 - c])
                for b in range(nz):
                    i = a * nz + b
                    w.inv[c][m, i] = jnp.where(inside(m, i), 1.0 / (diag[c][b] + high[b]), 0.0)

        for a in range(ny):
            rows = [load(w.b[c], m, a) for c in (0, 1)]
            rolled = [up_rolled(rows[c]) for c in (0, 1)]
            low_y = [[p + q for p, q in zip(rows[c], from_above(last[1 - c], rolled[1 - c]))] for c in (0, 1)]
            last = rolled
            low_z = [[p + q for p, q in zip(rows[c], from_left(rows[1 - c]))] for c in (0, 1)]
            diag = []
            for c in (0, 1):
                high_z = from_right(low_z[1 - c])
                total = []
                for b in range(nz):
                    i = a * nz + b
                    x_in = rows[0][b] + rows[1][b]
                    lower, upper = w.b[1 - c][before, i], w.b[1 - c][after, i]
                    x_out = rows[c][b] + (jnp.where(even, lower, upper) if c == 0 else jnp.where(even, upper, lower))
                    if c == 0:
                        w.x_in[m, i] = x_in
                    w.x_out[c][m, i] = x_out
                    w.y[c][m, i] = low_y[c][b]
                    w.z[c][m, i] = low_z[c][b]
                    total.append((x_in + x_out) + low_y[c][b] + (low_z[c][b] + high_z[b]))
                diag.append(total)
            here = [down_rolled(low_y[c]) for c in (0, 1)]
            if a == 0:
                first = here
            else:
                finish(a - 1, waiting[0], waiting[1], here)
            waiting = (diag, here)
        finish(ny - 1, waiting[0], waiting[1], first)
        return 0

    lax.fori_loop(0, PAIRS, body, 0, unroll=2)


def smooth_level(w, ny, nz):
    up_rolled, down_rolled, from_above, from_below, from_left, from_right, load = level_helpers(ny, nz)
    even = lax.rem(iota(0) + iota(1), 2) == 0

    for half in range(2 * SWEEPS):
        c = half % 2
        old, new = w.e[1 - c], w.e[c]

        def body(m, _, c=c, old=old, new=new):
            before, after = jnp.maximum(m - 1, 0), jnp.minimum(m + 1, PAIRS - 1)

            def lowered(a, row):
                return down_rolled([p * q for p, q in zip(load(w.y[1 - c], m, a), row)])

            last = up_rolled(load(old, m, ny - 1))
            row = load(old, m, 0)
            here = first = lowered(0, row)
            for a in range(ny):
                rolled = up_rolled(row)
                up = from_above(last, rolled)
                if a + 1 < ny:
                    row_next = load(old, m, a + 1)
                    edge = lowered(a + 1, row_next)
                else:
                    row_next, edge = None, first
                down = from_below(edge, here)
                left = from_left(row)
                right = from_right([p * q for p, q in zip(load(w.z[1 - c], m, a), row)])
                for b in range(nz):
                    i = a * nz + b
                    lower, upper = old[before, i], old[after, i]
                    far = jnp.where(even, lower, upper) if c == 0 else jnp.where(even, upper, lower)
                    off = w.x_in[m, i] * row[b] + w.x_out[c][m, i] * far
                    off = off + (w.y[c][m, i] * up[b] + down[b]) + (w.z[c][m, i] * left[b] + right[b])
                    new[m, i] = (w.r[c][m, i] + off) * w.inv[c][m, i]
                last, row, here = rolled, row_next, edge
            return 0

        skip = (half + 1) // 2
        lax.fori_loop(skip, PAIRS - skip, body, 0, unroll=4)


class Level:
    def __init__(self, refs):
        refs = list(refs)
        self.x_in = refs[0]
        self.e, self.r, self.b, self.x_out, self.y, self.z, self.inv = (refs[1 + 2 * i : 3 + 2 * i] for i in range(7))


def smooth_kernel(window, down, up, nxt, prv, far, out_fine, out_coarse, *scratch):
    gx, gy, gz = lax.axis_index("gx"), lax.axis_index("gy"), lax.axis_index("gz")
    lane, sub = iota(1), iota(0)
    even = lax.rem(lane + sub, 2) == 0
    mid, fine = Level(scratch[:15]), Level(scratch[15:])

    def place(ref, base, n, level, pair0, pairs, half=0.5):
        def copy(p, _):
            at = base + p * 4 * n
            for i in range(n):
                for kind, dest, scale in ((0, level.r, None), (1, level.b, half)):
                    one, two = ref[at + kind * n + i], ref[at + 2 * n + kind * n + i]
                    if scale is not None:
                        one, two = scale * one, scale * two
                    dest[0][pair0 + p, i] = jnp.where(even, one, two)
                    dest[1][pair0 + p, i] = jnp.where(even, two, one)
            return 0

        lax.fori_loop(0, pairs, copy, 0)

    place(far, 0, MT, mid, 0, 1, jnp.where(gx >= 2, 0.5, 0.0))
    place(prv, F_SEND, MT, mid, 1, 2)
    place(down, F_SEND, MT, mid, 3, 2)
    place(nxt, F_SEND, MT, mid, 5, 2)
    place(far, 0, MT, mid, 7, 1, jnp.where(gx < 2, 0.5, 0.0))
    place(prv, 0, FT, fine, 0, 2)
    place(down, 0, FT, fine, 2, 2)
    place(up, 0, FT, fine, 4, 2)
    place(nxt, 0, FT, fine, 6, 2)

    everywhere = jnp.full(VREG, True)
    in_z = ((lane < 64) & (gz < 15)) | ((lane >= 64) & (gz > 0))
    in_y = ((sub < 4) & (gy < 3)) | ((sub >= 4) & (gy > 0))

    def inside_x(m, first, size):
        return (2 * m + first >= 0) & (2 * m + first < size)

    def mid_inside(m, i):
        yt, zt = i // MZ, i % MZ
        y = everywhere if yt < 2 else jnp.full(VREG, gy < 3 if yt == 2 else gy > 0)
        return y & (everywhere if zt < 2 else in_z) & inside_x(m, 4 * gx - 6, 16)

    def fine_inside(m, i):
        yt, zt = i // FZ, i % FZ
        return (in_y if yt == 4 else everywhere) & (in_z if zt == 4 else everywhere) & inside_x(m, 8 * gx - 4, 32)

    prepare_level(mid, MY, MZ, mid_inside)
    prepare_level(fine, FY, FZ, fine_inside)

    src = lax.broadcasted_iota(jnp.int32, (256, 512), 0)
    dst = lax.broadcasted_iota(jnp.int32, (256, 512), 1)
    cell = 16 * (src % 16 - 2) + src // 16
    lanes = jnp.where(dst >= 320, dst - 384, dst)
    wanted = jnp.where(dst >= 384, dst - 384, (lanes + 128) // 2 - 64)
    pick = (cell == wanted).astype(F32)
    source = jnp.concatenate(
        [
            jnp.concatenate([window[i, tile, 0], window[i, tile, 1]], axis=1)
            for i in range(8)
            for tile in range(3)
        ],
        axis=0,
    )
    wide = jnp.dot(source, pick, precision=lax.Precision.HIGHEST, preferred_element_type=F32)

    def tile_of(i, tile, zt):
        row = (i * 3 + tile) * 8
        return wide[row : row + 8, zt * 128 : zt * 128 + 128]

    for i in range(2):
        out_coarse[i] = tile_of(3 + i, 0, 3)

    def doubled_rows(a, half):
        return jnp.take_along_axis(a, sub // 2 + 4 * half, axis=0, mode="promise_in_bounds")

    def doubled_lanes(a, half):
        return jnp.take_along_axis(a, lane // 2 + 64 * half, axis=1, mode="promise_in_bounds")

    for i in range(8):
        for zt in range(MZ):
            plane = [
                doubled_rows(tile_of(i, 0, zt), 0),
                doubled_rows(tile_of(i, 0, zt), 1),
                doubled_rows(tile_of(i, 1, zt), 0),
                doubled_rows(tile_of(i, 2, zt), 1),
            ]
            for yt in range(MY):
                mid.e[1][i, yt * MZ + zt] = jnp.where(mid_inside(i, yt * MZ + zt), plane[yt], 0.0)

    smooth_level(mid, MY, MZ)

    def prolong(pair, _):
        for odd in range(2):
            plane = []
            for b in range(MZ):
                src = []
                for a in range(MY):
                    red, black = (mid.e[c][pair + 2, a * MZ + b] for c in (0, 1))
                    src.append(jnp.where(even, black, red) if odd else jnp.where(even, red, black))
                edge = jnp.where(sub < 4, doubled_rows(src[2], 0), doubled_rows(src[3], 1))
                plane.append([doubled_rows(src[a // 2], a % 2) for a in range(4)] + [edge])
            for a in range(FY):
                row = [doubled_lanes(plane[b // 2][a], b % 2) for b in range(4)]
                last = plane[2][a]
                row.append(jnp.where(lane < 64, doubled_lanes(last, 0), doubled_lanes(last, 1)))
                for b in range(FZ):
                    fine.e[1][2 * pair + odd, a * FZ + b] = row[b]
        return 0

    lax.fori_loop(0, 4, prolong, 0, unroll=4)
    smooth_level(fine, FY, FZ)

    def store(p, _):
        for a in range(4):
            for b in range(4):
                red, black = (fine.e[c][p + 2, a * FZ + b] for c in (0, 1))
                out_fine[2 * p, a * 8 : a * 8 + 8, b * 128 : b * 128 + 128] = jnp.where(even, red, black)
                out_fine[2 * p + 1, a * 8 : a * 8 + 8, b * 128 : b * 128 + 128] = jnp.where(even, black, red)
        return 0

    lax.fori_loop(0, 4, store, 0, unroll=4)


def smooth(window, *parts):
    mid = pltpu.VMEM((PAIRS, MT) + VREG, F32)
    fine = pltpu.VMEM((PAIRS, FT) + VREG, F32)
    return pl.pallas_call(
        smooth_kernel,
        out_shape=(jax.ShapeDtypeStruct((8, 32, 512), F32), jax.ShapeDtypeStruct((2,) + VREG, F32)),
        scratch_shapes=[mid] * 15 + [fine] * 15,
        compiler_params=params(48),
        name="smooth",
    )(window, *parts)


def send(a, axis, step):
    n = lax.axis_size(axis)
    return lax.ppermute(a, axis, [(i, i + step) for i in range(n) if 0 <= i + step < n])


def shards(rhs_fine, beta_fine, rhs_mid, beta_mid, rhs_coarse, beta_coarse):
    fine, mid = [rhs_fine, beta_fine], [rhs_mid, beta_mid]
    y_first, y_last, blocks = pack(fine, mid, [rhs_coarse, beta_coarse])
    y_next, y_prev = send(y_first, "gy", -1), send(y_last, "gy", 1)
    col = column(lax.all_to_all(blocks, "gz", 0, 0))
    parts = gather(col, True)
    yh, z_first, z_last = pack_z(fine, mid, y_next, y_prev)
    parts, z_first, z_last = lax.optimization_barrier((parts, z_first, z_last))
    z_next, z_prev = send(z_first, "gz", -1), send(z_last, "gz", 1)
    parts = gather(join(parts, True), False)
    parts, z_next, z_prev = lax.optimization_barrier((parts, z_next, z_prev))
    own = join(parts, False)
    other = lax.ppermute(own, "gz", [(i, i ^ 1) for i in range(16)])
    down, up, across = pack_x(fine, mid, yh, z_next, z_prev)
    x_next, x_prev = send(down, "gx", -1), send(up, "gx", 1)
    x_far = lax.ppermute(across, "gx", [(i, (i + 2) % 4) for i in range(4)])
    window = solve(own, other)
    return smooth(window, down, up, x_next, x_prev, x_far)


def solution(mesh):
    spec = P("gx", "gy", "gz")
    return jax.shard_map(
        shards, mesh=mesh, in_specs=(spec,) * 6, out_specs=(spec, spec), check_vma=False
    )
```
